512 devices in a mesh: kv: 8 (over y, core), req: 64 (over z, x).
Axes of the slice: x: 4, y: 4, z: 16, core: 2. Of those that a mesh axis runs over, the one named last changes fastest.
Arguments:
- queries: bfloat16 [2048, 4, 64, 128], P('req', None, 'kv'), may hold values from -4.8125 to 4.8125
- new_keys: bfloat16 [2048, 4, 8, 128], P('req', None, 'kv'), may hold values from -4.8125 to 4.8125
- new_values: bfloat16 [2048, 4, 8, 128], P('req', None, 'kv'), may hold values from -6 to 6
- suffix_keys: bfloat16 [2048, 128, 8, 128], P('req', None, 'kv'), may hold values from -4.8125 to 4.8125
- suffix_values: bfloat16 [2048, 128, 8, 128], P('req', None, 'kv'), may hold values from -6 to 6
- suffix_len: int32 [2048], P('req'), may hold values from 1 to 128, 229376 in all
- block_table: int32 [2048, 4], P('req'), may hold values from 0 to 127, all different within a row; in each aligned block of 32 rows (0 to 31, 32 to 63, ...) at most 2 rows name the same one
- prefix_keys: bfloat16 [128, 1024, 8, 128], P('req', None, 'kv'), may hold values from -4.8125 to 4.8125
- prefix_values: bfloat16 [128, 1024, 8, 128], P('req', None, 'kv'), may hold values from -6 to 6
Outputs:
- attended: bfloat16 [256, 8, 4, 8192], P('req', 'kv')
The draws below stay inside these ranges and needn't reach their ends.
Inputs may be any that keep to these rules, and one draw needn't show every extreme that they name: `block_table`: among the 32 requests of one device (aligned blocks of rows) no span is named by more than 2 requests, a bound that some block reaches; a request names 4 different spans.
All inputs are finite; a program needn't handle non-finite values. No bound on the sum of `suffix_len` on one device may be relied on, other than what follows from the above.
Results may differ from the reference program's by a relative error of at most 0.0046.
Values may be sent and summed in bfloat16 or wider, within the bound.
No kernel may reach another device: no remote copies, remote signals or barrier semaphores. Data moves between devices by JAX's collectives and lax.ppermute only.
A program may use at most 64 MiB of HBM per device.

```python
import math
import jax
import jax.numpy as jnp
import numpy as np
from jax import lax

HD = 128
QH_ALL = 64
KVH = 8
GROUP = 8
REQ_DEV = 32
STEPS = 4
SPAN = 1024
DEPTH = 4
SUF = 128
REQUESTS = 2048
NCHUNKS = 128
CAP = 2
N_KV = 8


def drawn_field(key, shape):
    return jnp.clip(jax.random.normal(key, shape, jnp.float32), -4.8, 4.8)


def draw_queries(key, part):
    key = jax.random.fold_in(key, 11)
    shape = (REQUESTS, STEPS, QH_ALL, HD)
    values = drawn_field(key, shape)
    return values.astype(jnp.bfloat16)


def draw_new_keys(key, part):
    key = jax.random.fold_in(key, 12)
    shape = (REQUESTS, STEPS, KVH, HD)
    values = drawn_field(key, shape)
    return values.astype(jnp.bfloat16)


def draw_suffix_keys(key, part):
    key = jax.random.fold_in(key, 13)
    shape = (REQUESTS, SUF, KVH, HD)
    values = drawn_field(key, shape)
    return values.astype(jnp.bfloat16)


def draw_prefix_keys(key, part):
    key = jax.random.fold_in(key, 14)
    shape = (NCHUNKS, SPAN, KVH, HD)
    values = drawn_field(key, shape)
    return values.astype(jnp.bfloat16)


def level_of(own_key, shape, cuts, low, high):
    loudness, own = 1.0, jax.random.fold_in(own_key, 6)
    for dim, blocks in cuts:
        heights = jnp.exp(jax.random.uniform(jax.random.fold_in(own, dim), (blocks,), jnp.float32, low / len(cuts), high / len(cuts)))
        loudness = loudness * jnp.repeat(heights, shape[dim] // blocks).reshape([-1 if axis == dim else 1 for axis in range(len(shape))])
    return loudness


def split_up(count, total, limit, skew):
    weights = [(1 << 20) // math.isqrt(rank ** skew) + 1 for rank in range(2, count + 1)]
    spare, holding = total - limit - (count - 1), [1] * (count - 1)
    while spare > 0:
        candidates = [i for i in range(count - 1) if holding[i] < limit]
        mass, budget = sum([weights[i] for i in candidates]), spare
        for i in candidates:
            addition = min(limit - holding[i], max(1, budget * weights[i] // mass), spare)
            holding[i] = holding[i] + addition
            spare = spare - addition
    return np.array([limit] + holding)


def uneven(key, amount, total, limit, lean):
    if amount == 2:
        one = jax.random.randint(key, (), max(1, total - limit), min(limit, total - 1) + 1)
        return jnp.stack([one, total - one])
    lengths = jnp.asarray(split_up(amount, total, limit, lean), jnp.int32)
    couples = (amount - 1) // 2
    giver, receiver = lengths[1:1 + 2 * couples:2], lengths[2:2 + 2 * couples:2]
    slack = jnp.minimum(giver - 1, limit - receiver)
    shifted = jax.random.randint(jax.random.fold_in(key, 1), (couples,), 0, 1 << 20) % (slack + 1)
    lengths = lengths.at[1:1 + 2 * couples:2].set(giver - shifted).at[2:2 + 2 * couples:2].set(receiver + shifted)
    return lengths[jax.random.permutation(jax.random.fold_in(key, 2), amount)]


def routed_block(own_key, own, number, rows, count, top, bound, skew):
    order = jax.random.permutation(own_key, count)
    heavy_load, ordinary = load_shares(count, rows * top, bound, skew, True), load_shares(count, rows * top, bound, skew, False)
    places = jnp.arange(count)

    def named(lengths, turn):
        used = int((lengths > 0).sum())
        fixed = max(1, used // 4)
        passed = fixed + (places - fixed + turn * (used - fixed)) % max(1, count - fixed)
        return jnp.zeros((count,), jnp.int32).at[order[jnp.where(places < fixed, places, passed)]].set(jnp.asarray(lengths, jnp.int32))

    lengths = jnp.where(number % 4 == 0, named(heavy_load, number // 4), named(ordinary, number - number // 4 - 1))
    mixed = jax.random.permutation(jax.random.fold_in(own, 3), count)
    giver, taker = mixed[0:count // 2 * 2:2], mixed[1:count // 2 * 2:2]
    slack = jnp.minimum(lengths[giver] - 1, bound - lengths[taker]) // 2
    slack = jnp.where((giver == order[0]) | (taker == order[0]) | (lengths[taker] == 0), 0, jnp.maximum(slack, 0))
    passed = jax.random.randint(jax.random.fold_in(own, 4), (count // 2,), 0, 1 << 20) % (slack + 1)
    lengths = lengths.at[giver].add(-passed).at[taker].add(passed)
    items = jnp.searchsorted(jnp.cumsum(lengths), jnp.arange(rows * top), side="right").astype(jnp.int32)
    table = items.reshape(top, rows).T
    table = table[jax.random.permutation(jax.random.fold_in(own, 1), rows)]
    turn = jax.random.randint(jax.random.fold_in(own, 2), (rows, 1), 0, top)
    return jnp.take_along_axis(table, (jnp.arange(top)[None, :] + turn) % top, axis=1)


def load_shares(amount, total, reach, lean, full):
    portions = [(1 << 20) // math.isqrt(rank ** lean) + 1 for rank in range(1, amount + 1)]
    largest = reach if full else min(reach, max(-(-total // amount), total * portions[0] // sum(portions)))
    least = 1 if total - largest >= amount - 1 else 0
    given, spare = [largest] + [least] * (amount - 1), total - largest - least * (amount - 1)
    while spare > 0:
        free = [i for i in range(1, amount) if given[i] < largest] or [i for i in range(1, amount) if given[i] < reach]
        whole, remaining = sum([portions[i] for i in free]), spare
        for i in free:
            more = min(reach - given[i], max(1, remaining * portions[i] // whole), spare)
            given[i] = given[i] + more
            spare = spare - more
    return np.array(given)


def scatter_about(own_key, extent, width, most, split=(), kind=jnp.bfloat16):
    values = jax.random.normal(own_key, extent, jnp.float32) * width
    if len(split) > 0:
        values = level_of(own_key, extent, split, -0.22, 0.18) * values
    return jnp.clip(values, min=-most, max=most).astype(kind)


def setup_inputs(seed: int = 0) -> dict:
    seeds = jax.random.split(jax.random.key(seed), 10)
    queries = draw_queries(jax.random.fold_in(seeds[9], 71), 0)
    new_keys = draw_new_keys(jax.random.fold_in(seeds[9], 71), 0)
    new_values = scatter_about(seeds[2], (REQUESTS, STEPS, KVH, HD), 1.0, 6.0, ((0, 64), (2, 8)))
    suffix_keys = draw_suffix_keys(jax.random.fold_in(seeds[9], 71), 0)
    suffix_values = scatter_about(seeds[4], (REQUESTS, SUF, KVH, HD), 1.0, 6.0, ((0, 64), (2, 8)))
    suffix_len = uneven(seeds[5], REQUESTS, REQUESTS * (7 * SUF // 8), SUF, 1).astype(jnp.int32)
    block_table_keys = jax.random.split(jax.random.fold_in(seeds[6], 1), REQUESTS // REQ_DEV)
    block_table_turns = jax.random.permutation(jax.random.fold_in(seeds[6], 3), REQUESTS // REQ_DEV)
    block_table = jax.vmap(lambda own, number: routed_block(jax.random.fold_in(seeds[6], 2), own, number, REQ_DEV, NCHUNKS, DEPTH, CAP, 2))(block_table_keys, block_table_turns).reshape((REQUESTS, DEPTH))
    prefix_keys = draw_prefix_keys(jax.random.fold_in(seeds[9], 71), 0)
    prefix_values = scatter_about(seeds[8], (NCHUNKS, SPAN, KVH, HD), 1.0, 6.0, ((0, 64), (2, 8)))
    return {"queries": queries, "new_keys": new_keys, "new_values": new_values, "suffix_keys": suffix_keys, "suffix_values": suffix_values, "suffix_len": suffix_len, "block_table": block_table, "prefix_keys": prefix_keys, "prefix_values": prefix_values}


def span_reference(grouped, key_block, value_block):
    scaling = HD ** -0.5
    scores = jnp.einsum("bsngd,btnd->bsngt", grouped.astype(jnp.float32), key_block.astype(jnp.float32)) * scaling
    highest = jnp.max(scores, axis=-1)
    weights = jnp.exp(scores - highest[..., None])
    summed = jnp.sum(weights, axis=-1)
    rounded = lax.optimization_barrier(weights.astype(jnp.bfloat16)).astype(jnp.float32)
    product = jnp.einsum("bsngt,btnd->bsngd", rounded, value_block.astype(jnp.float32))
    return product / summed[..., None], highest + jnp.log(summed)


def own_reference(grouped, cache_keys, cache_values, fresh_keys, fresh_values, live_len):
    scaling = HD ** -0.5
    query_f = grouped.astype(jnp.float32)
    cache_scores = jnp.einsum("rsngd,rtnd->rsngt", query_f, cache_keys.astype(jnp.float32)) * scaling
    fresh_scores = jnp.einsum("rsngd,rtnd->rsngt", query_f, fresh_keys.astype(jnp.float32)) * scaling
    cache_live = jnp.arange(SUF, dtype=jnp.int32)[None, :] < live_len[:, None]
    cache_scores = jnp.where(cache_live[:, None, None, None, :], cache_scores, -1e30)
    causal = jnp.arange(STEPS, dtype=jnp.int32)[None, :] <= jnp.arange(STEPS, dtype=jnp.int32)[:, None]
    fresh_scores = jnp.where(causal[None, :, None, None, :], fresh_scores, -1e30)
    highest = jnp.maximum(jnp.max(cache_scores, axis=-1), jnp.max(fresh_scores, axis=-1))
    cache_w = jnp.exp(cache_scores - highest[..., None])
    fresh_w = jnp.exp(fresh_scores - highest[..., None])
    summed = jnp.sum(cache_w, axis=-1) + jnp.sum(fresh_w, axis=-1)
    cache_r = lax.optimization_barrier(cache_w.astype(jnp.bfloat16)).astype(jnp.float32)
    fresh_r = lax.optimization_barrier(fresh_w.astype(jnp.bfloat16)).astype(jnp.float32)
    product = jnp.einsum("rsngt,rtnd->rsngd", cache_r, cache_values.astype(jnp.float32))
    product = product + jnp.einsum("rsngt,rtnd->rsngd", fresh_r, fresh_values.astype(jnp.float32))
    return product / summed[..., None], highest + jnp.log(summed)


def merge_states(partials, log_sums, axis_pos):
    ceiling = jnp.max(log_sums, axis=axis_pos, keepdims=True)
    factors = jnp.exp(log_sums - ceiling)
    weighted = jnp.sum(factors[..., None] * partials, axis=axis_pos)
    return (weighted / jnp.sum(factors, axis=axis_pos)[..., None]).astype(jnp.bfloat16)


def reference(queries, new_keys, new_values, suffix_keys, suffix_values, suffix_len, block_table, prefix_keys, prefix_values):
    batch_rows = 8

    def per_block(pieces):
        block_q, block_nk, block_nv, block_sk, block_sv, block_len, block_rows = pieces
        grouped = block_q.reshape(batch_rows, STEPS, KVH, GROUP, HD)
        part_list = []
        log_list = []
        for level in range(DEPTH):
            picked = block_rows[:, level]
            mixed, logs = span_reference(grouped, prefix_keys[picked], prefix_values[picked])
            part_list.append(mixed)
            log_list.append(logs)
        mixed, logs = own_reference(grouped, block_sk, block_sv, block_nk, block_nv, block_len)
        part_list.append(mixed)
        log_list.append(logs)
        partials = jnp.stack(part_list, axis=1).reshape(batch_rows, DEPTH + 1, STEPS, QH_ALL, HD)
        log_sums = jnp.stack(log_list, axis=1).reshape(batch_rows, DEPTH + 1, STEPS, QH_ALL)
        return merge_states(partials, log_sums, 1)

    inputs = (queries, new_keys, new_values, suffix_keys, suffix_values, suffix_len, block_table)
    stacked = tuple(item.reshape((REQUESTS // batch_rows, batch_rows) + item.shape[1:]) for item in inputs)
    result = lax.map(per_block, stacked)
    return result.reshape(REQUESTS // N_KV, N_KV, STEPS, QH_ALL * HD)
```

```python
import jax
import jax.numpy as jnp
from jax import lax
from jax.experimental import pallas as pl
from jax.experimental.pallas import tpu as pltpu
from jax.sharding import PartitionSpec as P

NX = 4
CAP = 2
CHUNKS = 2
TILE = 256
PAD = 16
EMPTY = -1e30


def dot(a, b, dims):
    return lax.dot_general(a, b, (dims, ((), ())), preferred_element_type=jnp.float32)


def three_parts(line):
    parts = []
    for _ in range(3):
        piece = line.astype(jnp.bfloat16)
        line = line - piece.astype(jnp.float32)
        parts.append(piece)
    return parts


def span_kernel(q_ref, k_ref, v_ref, out_ref, logs_ref):
    spans, rows, width = q_ref.shape[1:]
    scale = width ** (-0.5)
    tile = min(TILE, rows)
    base = spans * rows
    blocks, lanes = logs_ref.shape[0] // 2, logs_ref.shape[1]
    per = rows // blocks
    logs_ref[...] = jnp.zeros_like(logs_ref)
    for s in range(spans):
        for t in range(0, rows, tile):
            q = q_ref[0, s, t : t + tile, :]
            scores = dot(k_ref[s], q, ((1,), (1,)))
            top = jnp.max(scores, axis=0, keepdims=True)
            weights = jnp.exp((scores - top) * scale)
            total = jnp.sum(weights, axis=0, keepdims=True)
            mixed = dot(v_ref[s], weights.astype(jnp.bfloat16), ((1,), (0,)))
            mixed = mixed / total
            at = s * rows + t
            out_ref[0, at : at + tile, :] = mixed.T.astype(jnp.bfloat16)
            parts = three_parts(top * scale + jnp.log(total))
            for u in range(0, tile, per):
                block = (t + u) // per
                for p in range(3):
                    line = blocks * (p // 2) + block
                    lane = (p % 2) * spans * per + s * per
                    logs_ref[line : line + 1, lane : lane + per] = parts[p][
                        :, u : u + per
                    ].astype(jnp.float32)
    out_ref[0, base : base + 2 * blocks, :] = logs_ref[...].astype(jnp.bfloat16)


def span_states(q, keys, values, blocks):
    peers, spans, rows, width = q.shape
    lines = spans * rows + 2 * blocks
    return pl.pallas_call(
        span_kernel,
        grid=(peers,),
        in_specs=[
            pl.BlockSpec((1, spans, rows, width), lambda i: (i, 0, 0, 0)),
            pl.BlockSpec(keys.shape, lambda i: (0, 0, 0)),
            pl.BlockSpec(values.shape, lambda i: (0, 0, 0)),
        ],
        out_specs=pl.BlockSpec((1, lines, width), lambda i: (i, 0, 0)),
        out_shape=jax.ShapeDtypeStruct((peers, lines, width), jnp.bfloat16),
        scratch_shapes=[pltpu.VMEM((2 * blocks, width), jnp.float32)],
        compiler_params=pltpu.CompilerParams(vmem_limit_bytes=48 * 1024 * 1024),
        cost_estimate=pl.CostEstimate(
            flops=4 * peers * spans * rows * keys.shape[1] * width,
            bytes_accessed=4 * peers * lines * width + 4 * keys.size,
            transcendentals=peers * spans * rows * keys.shape[1],
        ),
    )(q, keys, values)


def as_columns(line):
    count = line.shape[1]
    return jnp.concatenate(
        [
            jnp.broadcast_to(line[:, u : u + 128], (128, 128)).T
            for u in range(0, count, 128)
        ],
        axis=0,
    )


def merge_slots(data_refs, logs, targets, arrived):
    peers = data_refs[0].shape[0]
    data = jnp.concatenate([ref[x] for x in range(peers) for ref in data_refs], axis=0)
    rows = arrived_rows(arrived)
    slots = data.shape[0]
    column = as_columns(logs)
    column = jnp.concatenate([column] * (rows // 128), axis=1)
    mask = lax.broadcasted_iota(jnp.int32, (slots, rows), 1) == targets
    top = jnp.max(jnp.where(mask, column, EMPTY), axis=0, keepdims=True)
    states = []
    for ref in arrived[1]:
        width = ref.shape[0] - PAD
        log = jnp.sum(ref[width:, :].astype(jnp.float32), axis=0, keepdims=True)
        states.append((ref[:width, :].astype(jnp.float32), log))
        top = jnp.maximum(top, log)
    weights = jnp.where(mask, jnp.exp(column - top), 0.0)
    total = jnp.sum(weights, axis=0, keepdims=True)
    high = weights.astype(jnp.bfloat16)
    low = (weights - high.astype(jnp.float32)).astype(jnp.bfloat16)
    out = dot(data, high, ((0,), (0,))) + dot(data, low, ((0,), (0,)))
    for state, log in states:
        factor = jnp.exp(log - top)
        total = total + factor
        out = out + state * factor
    total = jnp.where(total == 0.0, 1.0, total)
    return out * (1.0 / total), top + jnp.log(total)


def arrived_rows(arrived):
    return arrived[0]


def step_kernel(rows, count, *refs):
    data_refs, logs_ref, targets_ref = refs[:2], refs[2], refs[3]
    out_ref = refs[-1]
    out, log = merge_slots(data_refs, logs_ref[0], targets_ref[0], (rows, refs[4 : 4 + count]))
    width = out.shape[0]
    out_ref[:width, :] = out.astype(jnp.bfloat16)
    parts = three_parts(log)
    rest = jnp.zeros((PAD - 3, rows), jnp.bfloat16)
    out_ref[width:, :] = jnp.concatenate(parts + [rest], axis=0)


def last_kernel(rows, count, *refs):
    data_refs, logs_ref, targets_ref = refs[:2], refs[2], refs[3]
    own_ref, own_log_ref, out_ref = refs[-3:]
    out, log = merge_slots(data_refs, logs_ref[0], targets_ref[0], (rows, refs[4 : 4 + count]))
    out = out.T
    log = as_columns(log)
    own_log = own_log_ref[...]
    top = jnp.maximum(log, own_log)
    far, near = jnp.exp(log - top), jnp.exp(own_log - top)
    merged = (far * out + near * own_ref[...]) / (far + near)
    out_ref[...] = merged.astype(jnp.bfloat16)


def merge_call(kernel, place, states, logs, targets, arrived, extra, rows, out_shape):
    peers, lines, width = states.shape
    blocks, _, slots = logs.shape
    group = slots // (2 * peers)

    def whole(a):
        return pl.BlockSpec(a.shape, lambda i, n=a.ndim: (0,) * n)

    return pl.pallas_call(
        lambda *refs: kernel(rows, len(arrived), *refs),
        grid=(1,),
        in_specs=[
            pl.BlockSpec((peers, group, width), lambda i: (0, place, 0)),
            pl.BlockSpec((peers, group, width), lambda i: (0, blocks + place, 0)),
            pl.BlockSpec((1, 1, slots), lambda i: (place, 0, 0)),
            pl.BlockSpec((1, slots, 1), lambda i: (place, 0, 0)),
        ]
        + [whole(a) for a in arrived + extra],
        out_specs=pl.BlockSpec(out_shape, lambda i: (0, 0)),
        out_shape=jax.ShapeDtypeStruct(out_shape, jnp.bfloat16),
        compiler_params=pltpu.CompilerParams(vmem_limit_bytes=32 * 1024 * 1024),
        cost_estimate=pl.CostEstimate(
            flops=4 * rows * slots * width,
            bytes_accessed=4 * rows * width,
            transcendentals=rows * slots,
        ),
    )(states, states, logs, targets, *arrived, *extra)


def own_states(grouped, cache_keys, cache_values, fresh_keys, fresh_values, live_len):
    scaling = grouped.shape[-1] ** (-0.5)
    step_count = grouped.shape[1]
    cache_slots = cache_keys.shape[1]
    cache_scores = (
        jnp.einsum("rsngd,rtnd->rsngt", grouped, cache_keys, preferred_element_type=jnp.float32)
        * scaling
    )
    fresh_scores = (
        jnp.einsum("rsngd,rtnd->rsngt", grouped, fresh_keys, preferred_element_type=jnp.float32)
        * scaling
    )
    cache_live = jnp.arange(cache_slots, dtype=jnp.int32)[None, :] < live_len[:, None]
    cache_scores = jnp.where(cache_live[:, None, None, None, :], cache_scores, EMPTY)
    causal = (
        jnp.arange(step_count, dtype=jnp.int32)[None, :]
        <= jnp.arange(step_count, dtype=jnp.int32)[:, None]
    )
    fresh_scores = jnp.where(causal[None, :, None, None, :], fresh_scores, EMPTY)
    highest = jnp.maximum(jnp.max(cache_scores, axis=-1), jnp.max(fresh_scores, axis=-1))
    cache_w = jnp.exp(cache_scores - highest[..., None])
    fresh_w = jnp.exp(fresh_scores - highest[..., None])
    summed = jnp.sum(cache_w, axis=-1) + jnp.sum(fresh_w, axis=-1)
    product = jnp.einsum(
        "rsngt,rtnd->rsngd",
        cache_w.astype(jnp.bfloat16),
        cache_values,
        preferred_element_type=jnp.float32,
    )
    product = product + jnp.einsum(
        "rsngt,rtnd->rsngd",
        fresh_w.astype(jnp.bfloat16),
        fresh_values,
        preferred_element_type=jnp.float32,
    )
    return (product / summed[..., None], highest + jnp.log(summed))


def local(
    queries,
    new_keys,
    new_values,
    suffix_keys,
    suffix_values,
    suffix_len,
    block_table,
    prefix_keys,
    prefix_values,
):
    requests, steps, heads, width = queries.shape
    span_count, span_len = prefix_keys.shape[:2]
    depth = block_table.shape[1]
    owners = lax.axis_size("req")
    nz = owners // NX
    half = nz // 2
    row = lax.axis_index("req") // NX
    z_groups = [[z * NX + x for z in range(nz)] for x in range(NX)]
    x_groups = [[z * NX + x for x in range(NX)] for z in range(nz)]
    keys = prefix_keys.reshape(span_count, span_len, width)
    values = prefix_values.reshape(span_count, span_len, width).transpose(0, 2, 1)

    def shift(array, by):
        pairs = [(z * NX + x, (z + by) % nz * NX + x) for z in range(nz) for x in range(NX)]
        return lax.ppermute(array, "req", pairs)

    per = steps // CHUNKS
    rows = per * heads
    pieces = []
    for c in range(CHUNKS):
        part = queries[:, c * per : (c + 1) * per].reshape(requests, rows, width)
        pieces.append({0: part})
    for k in range(1, half + 1):
        for c in range(CHUNKS):
            pieces[c][k] = shift(pieces[c][k - 1], -1)
            if k < half:
                pieces[c][nz - k] = shift(pieces[c][(nz - k + 1) % nz], 1)

    table = jnp.broadcast_to(block_table.reshape(1, -1), (nz, requests * depth))
    table = lax.all_to_all(
        table, "req", split_axis=0, concat_axis=0, tiled=True, axis_index_groups=z_groups
    )
    table = jnp.concatenate([table, table], axis=0)
    table = lax.dynamic_slice_in_dim(table, row, nz, 0).reshape(nz, requests, depth)
    here = row * NX * span_count + jnp.arange(NX * span_count, dtype=jnp.int32)
    match = jnp.any(table[None] == here[:, None, None, None], axis=-1)
    who = jnp.arange(requests, dtype=jnp.int32)
    first = jnp.min(jnp.where(match, who, requests), axis=-1)
    last = jnp.max(jnp.where(match, who, -1), axis=-1)
    chosen = jnp.stack(
        [jnp.where(last >= 0, first, -1), jnp.where(last > first, last, -1)], axis=-1
    )
    block_at = (jnp.arange(nz, dtype=jnp.int32) * requests)[None, :, None]
    pick = (jnp.maximum(chosen, 0) + block_at).reshape(NX, span_count, nz, CAP)
    slot_req = chosen.transpose(1, 0, 2).reshape(nz, NX * span_count * CAP)
    slots = NX * span_count * CAP * rows
    targets = slot_req[:, :, None] * rows + jnp.arange(rows, dtype=jnp.int32)
    targets = jnp.where(slot_req[:, :, None] >= 0, targets, -1).reshape(nz, slots, 1)

    kv_local = new_keys.shape[2]
    grouped = queries.reshape(requests, steps, kv_local, heads // kv_local, width)
    own_part, own_log = own_states(
        grouped, suffix_keys, suffix_values, new_keys, new_values, suffix_len
    )
    own_part = own_part.reshape(requests, steps, heads, width)
    own_log = jnp.broadcast_to(
        own_log.reshape(requests, steps, heads, 1), (requests, steps, heads, width)
    )

    state_shape = (width + PAD, requests * rows)
    flat = requests * rows
    all_states = []
    all_logs = []
    for c in range(CHUNKS):
        pool = jnp.concatenate([pieces[c][g] for g in range(nz)], axis=0)
        outgoing = pool[pick].reshape(NX, span_count * nz * CAP * rows, width)
        incoming = lax.all_to_all(
            outgoing, "req", split_axis=0, concat_axis=0, tiled=True, axis_index_groups=x_groups
        )
        incoming = incoming.reshape(NX, span_count, nz * CAP * rows, width)
        states = span_states(incoming, keys, values, nz)
        states = lax.all_to_all(
            states, "req", split_axis=0, concat_axis=0, tiled=True, axis_index_groups=x_groups
        )
        base = span_count * nz * CAP * rows
        lanes = span_count * CAP * rows
        logs = states[:, base:].reshape(NX, 2, nz, width).astype(jnp.float32)
        logs = logs[:, 0, :, :lanes] + logs[:, 0, :, lanes : 2 * lanes] + logs[:, 1, :, :lanes]
        logs = logs.transpose(1, 0, 2).reshape(nz, 1, slots)
        all_states.append(states)
        all_logs.append(logs)

    def step(c, place, arrived):
        return merge_call(
            step_kernel, place, all_states[c], all_logs[c], targets, arrived, [], flat, state_shape
        )

    down = [step(c, half, []) for c in range(CHUNKS)]
    up = [step(c, half - 1, []) for c in range(CHUNKS)]
    for k in range(half - 1, -1, -1):
        for c in range(CHUNKS):
            down[c] = shift(down[c], -1)
            if k > 0:
                down[c] = step(c, nz - k, [down[c]])
                up[c] = shift(up[c], 1)
                if k > 1:
                    up[c] = step(c, k - 1, [up[c]])
    kv_count = lax.axis_size("kv")
    results = []
    for c in range(CHUNKS):
        own_p = own_part[:, c * per : (c + 1) * per].reshape(flat, width)
        own_l = own_log[:, c * per : (c + 1) * per].reshape(flat, width)
        merged = merge_call(
            last_kernel, 0, all_states[c], all_logs[c], targets,
            [down[c], up[c]], [own_p, own_l], flat, (flat, width),
        )
        results.append(merged.reshape(requests // kv_count, kv_count, per, heads * width))
    merged = jnp.concatenate(results, axis=2)
    return lax.all_to_all(merged, "kv", split_axis=1, concat_axis=3, tiled=True)


def solution(mesh):
    placed = (
        P("req", None, "kv", None),
        P("req", None, "kv", None),
        P("req", None, "kv", None),
        P("req", None, "kv", None),
        P("req", None, "kv", None),
        P("req"),
        P("req", None),
        P("req", None, "kv", None),
        P("req", None, "kv", None),
    )
    return jax.shard_map(
        local, mesh=mesh, in_specs=placed, out_specs=P("req", "kv", None, None), check_vma=False
    )
```

```python
import jax
import jax.numpy as jnp
from jax import lax
from jax.experimental import pallas as pl
from jax.experimental.pallas import tpu as pltpu
from jax.sharding import PartitionSpec as P

NX = 4
CAP = 2
PLAN = ("direct", "direct")
TILE = 256
PAD = 8
LOG2E = 1.4426950408889634
EMPTY = -1e30


def dot(a, b, dims):
    return lax.dot_general(a, b, (dims, ((), ())), preferred_element_type=jnp.float32)


def three_parts(line):
    parts = []
    for _ in range(3):
        piece = line.astype(jnp.bfloat16).astype(jnp.float32)
        line = line - piece
        parts.append(piece)
    return parts


def span_kernel(axis, q_ref, k_ref, v_ref, out_ref, logs_ref):
    blocks, lines = out_ref.shape[0], out_ref.shape[2]
    spans, per, width = q_ref.shape[2:]
    scale = width ** (-0.5)
    group = max(1, min(TILE // per, blocks))
    logs_ref[...] = jnp.zeros_like(logs_ref)
    for s in range(spans):
        for b in range(0, blocks, group):
            if axis == 0:
                q = q_ref[0, b : b + group, s]
            else:
                q = q_ref[b : b + group, 0, s]
            scores = dot(k_ref[s], q.reshape(group * per, width), ((1,), (1,)))
            top = jnp.max(scores, axis=0, keepdims=True)
            weights = jnp.exp2((scores - top) * (scale * LOG2E))
            total = jnp.sum(weights, axis=0, keepdims=True)
            mixed = dot(v_ref[s], weights.astype(jnp.bfloat16), ((1,), (0,)))
            mixed = (mixed * (1.0 / total)).T.astype(jnp.bfloat16)
            out_ref[b : b + group, 0, s * per : (s + 1) * per, :] = mixed.reshape(
                group, per, width
            )
            parts = three_parts(top * scale + jnp.log(total))
            for u in range(group):
                for p in range(3):
                    lane = (p % 2) * spans * per + s * per
                    logs_ref[b + u, p // 2 : p // 2 + 1, lane : lane + per] = parts[p][
                        :, u * per : (u + 1) * per
                    ]
    out_ref[:, 0, spans * per :, :] = logs_ref[...].astype(jnp.bfloat16)


def span_states(q, keys, values, axis):
    peers, blocks = (q.shape[0], q.shape[1]) if axis == 0 else (q.shape[1], q.shape[0])
    spans, per, width = q.shape[2:]
    lines = spans * per + PAD
    if axis == 0:
        q_spec = pl.BlockSpec((1, blocks, spans, per, width), lambda i: (i, 0, 0, 0, 0))
    else:
        q_spec = pl.BlockSpec((blocks, 1, spans, per, width), lambda i: (0, i, 0, 0, 0))
    return pl.pallas_call(
        lambda *refs: span_kernel(axis, *refs),
        grid=(peers,),
        in_specs=[
            q_spec,
            pl.BlockSpec(keys.shape, lambda i: (0, 0, 0)),
            pl.BlockSpec(values.shape, lambda i: (0, 0, 0)),
        ],
        out_specs=pl.BlockSpec((blocks, 1, lines, width), lambda i: (0, i, 0, 0)),
        out_shape=jax.ShapeDtypeStruct((blocks, peers, lines, width), jnp.bfloat16),
        scratch_shapes=[pltpu.VMEM((blocks, PAD, width), jnp.float32)],
        compiler_params=pltpu.CompilerParams(vmem_limit_bytes=48 * 1024 * 1024),
        cost_estimate=pl.CostEstimate(
            flops=4 * q.size * keys.shape[1],
            bytes_accessed=4 * q.size + 4 * keys.size,
            transcendentals=q.size // width * keys.shape[1],
        ),
    )(q, keys, values)


def named_by(table, spans):
    requests = table.shape[-2]
    match = jnp.any(table[None] == spans.reshape((-1,) + (1,) * table.ndim), axis=-1)
    who = jnp.arange(requests, dtype=jnp.int32)
    first = jnp.min(jnp.where(match, who, requests), axis=-1)
    last = jnp.max(jnp.where(match, who, -1), axis=-1)
    return jnp.stack(
        [jnp.where(last >= 0, first, -1), jnp.where(last > first, last, -1)], axis=-1
    )


def own_states(grouped, cache_keys, cache_values, fresh_keys, fresh_values, live_len):
    scaling = grouped.shape[-1] ** (-0.5)
    step_count = grouped.shape[1]
    cache_slots = cache_keys.shape[1]
    cache_scores = (
        jnp.einsum("rsngd,rtnd->rsngt", grouped, cache_keys, preferred_element_type=jnp.float32)
        * scaling
    )
    fresh_scores = (
        jnp.einsum("rsngd,rtnd->rsngt", grouped, fresh_keys, preferred_element_type=jnp.float32)
        * scaling
    )
    cache_live = jnp.arange(cache_slots, dtype=jnp.int32)[None, :] < live_len[:, None]
    cache_scores = jnp.where(cache_live[:, None, None, None, :], cache_scores, EMPTY)
    causal = (
        jnp.arange(step_count, dtype=jnp.int32)[None, :]
        <= jnp.arange(step_count, dtype=jnp.int32)[:, None]
    )
    fresh_scores = jnp.where(causal[None, :, None, None, :], fresh_scores, EMPTY)
    highest = jnp.maximum(jnp.max(cache_scores, axis=-1), jnp.max(fresh_scores, axis=-1))
    cache_w = jnp.exp(cache_scores - highest[..., None])
    fresh_w = jnp.exp(fresh_scores - highest[..., None])
    summed = jnp.sum(cache_w, axis=-1) + jnp.sum(fresh_w, axis=-1)
    product = jnp.einsum(
        "rsngt,rtnd->rsngd",
        cache_w.astype(jnp.bfloat16),
        cache_values,
        preferred_element_type=jnp.float32,
    )
    product = product + jnp.einsum(
        "rsngt,rtnd->rsngd",
        fresh_w.astype(jnp.bfloat16),
        fresh_values,
        preferred_element_type=jnp.float32,
    )
    return (product / summed[..., None], highest + jnp.log(summed))


def local(
    queries,
    new_keys,
    new_values,
    suffix_keys,
    suffix_values,
    suffix_len,
    block_table,
    prefix_keys,
    prefix_values,
):
    requests, steps, heads, width = queries.shape
    span_count, span_len = prefix_keys.shape[:2]
    depth = block_table.shape[1]
    owners = lax.axis_size("req")
    nz = owners // NX
    row = lax.axis_index("req") // NX
    z_groups = [[z * NX + x for z in range(nz)] for x in range(NX)]
    x_groups = [[z * NX + x for x in range(NX)] for z in range(nz)]
    keys = prefix_keys.reshape(span_count, span_len, width)
    values = prefix_values.reshape(span_count, span_len, width).transpose(0, 2, 1)
    per = steps // len(PLAN)
    rows = per * heads
    lines = span_count * CAP * rows

    chosen = named_by(block_table, jnp.arange(owners * span_count, dtype=jnp.int32))
    own_pick = jnp.maximum(chosen, 0).reshape(-1)
    second = chosen[:, 0][block_table] != jnp.arange(requests, dtype=jnp.int32)[:, None]
    slot_ids = block_table * CAP + second.astype(jnp.int32)

    arrived = []
    for c, how in enumerate(PLAN):
        part = queries[:, c * per : (c + 1) * per].reshape(requests, rows, width)
        if how == "direct":
            outgoing = part[own_pick].reshape(owners, lines, width)
            incoming = lax.all_to_all(
                outgoing, "req", split_axis=0, concat_axis=0, tiled=True
            )
            incoming = incoming.reshape(nz, NX, span_count, CAP * rows, width)
            arrived.append((incoming, 1))
            continue
        line = block_table.astype(jnp.bfloat16).reshape(1, -1)
        line = jnp.pad(line, ((0, rows - 1), (0, width - requests * depth)))
        pool = jnp.concatenate([part.reshape(-1, width), line], axis=0)
        pool = lax.all_gather(pool, "req", axis_index_groups=z_groups, tiled=True)
        pool = pool.reshape(nz, requests + 1, rows, width)
        table = pool[:, requests, 0, : requests * depth].astype(jnp.int32)
        here = row * NX * span_count + jnp.arange(NX * span_count, dtype=jnp.int32)
        picked = jnp.maximum(named_by(table.reshape(nz, requests, depth), here), 0)
        block_at = jnp.arange(nz, dtype=jnp.int32) * (requests + 1)
        picked = picked + block_at[None, :, None]
        picked = picked.reshape(NX, span_count, nz, CAP).transpose(0, 2, 1, 3).reshape(-1)
        outgoing = pool.reshape(nz * (requests + 1), rows, width)[picked]
        outgoing = outgoing.reshape(NX, nz * lines, width)
        incoming = lax.all_to_all(
            outgoing, "req", split_axis=0, concat_axis=0, tiled=True, axis_index_groups=x_groups
        )
        arrived.append((incoming.reshape(NX, nz, span_count, CAP * rows, width), 0))

    kv_local = new_keys.shape[2]
    grouped = queries.reshape(requests, steps, kv_local, heads // kv_local, width)
    own_part, own_log = own_states(
        grouped, suffix_keys, suffix_values, new_keys, new_values, suffix_len
    )
    own_part = own_part.reshape(requests, steps, heads, width)
    own_log = own_log.reshape(requests, steps, heads)

    kv_count = lax.axis_size("kv")
    results = []
    for c, (incoming, axis) in enumerate(arrived):
        states = span_states(incoming, keys, values, axis)
        states = states.reshape(owners, lines + PAD, width)
        if c + 1 < len(arrived) and PLAN[c + 1] == "direct":
            states, following = lax.optimization_barrier((states, arrived[c + 1][0]))
            arrived[c + 1] = (following, arrived[c + 1][1])
        states = lax.all_to_all(states, "req", split_axis=0, concat_axis=0, tiled=True)
        logs = states[:, lines : lines + 2].astype(jnp.float32)
        logs = logs[:, 0, :lines] + logs[:, 0, lines : 2 * lines] + logs[:, 1, :lines]
        logs = logs.reshape(owners * span_count * CAP, rows)[slot_ids]
        parts = states[:, :lines].reshape(owners * span_count * CAP, rows, width)[slot_ids]
        own_l = own_log[:, c * per : (c + 1) * per].reshape(requests, 1, rows)
        own_p = own_part[:, c * per : (c + 1) * per].reshape(requests, rows, width)
        top = jnp.maximum(jnp.max(logs, axis=1, keepdims=True), own_l)
        factors = jnp.exp(logs - top)
        own_f = jnp.exp(own_l - top)[:, 0]
        total = jnp.sum(factors, axis=1) + own_f
        merged = jnp.sum(factors[..., None] * parts.astype(jnp.float32), axis=1)
        merged = (merged + own_f[..., None] * own_p) / total[..., None]
        merged = merged.astype(jnp.bfloat16)
        merged = merged.reshape(requests // kv_count, kv_count, per, heads * width)
        results.append(lax.all_to_all(merged, "kv", split_axis=1, concat_axis=3, tiled=True))
    return jnp.concatenate(results, axis=2)


def solution(mesh):
    placed = (
        P("req", None, "kv", None),
        P("req", None, "kv", None),
        P("req", None, "kv", None),
        P("req", None, "kv", None),
        P("req", None, "kv", None),
        P("req"),
        P("req", None),
        P("req", None, "kv", None),
        P("req", None, "kv", None),
    )
    return jax.shard_map(
        local, mesh=mesh, in_specs=placed, out_specs=P("req", "kv", None, None), check_vma=False
    )
```

```python
import jax
import jax.numpy as jnp
from jax import lax
from jax.experimental import pallas as pl
from jax.experimental.pallas import tpu as pltpu
from jax.sharding import PartitionSpec as P

NX = 4
CAP = 2
ROOM = 11
CHUNKS = 2
TILE = 256
PAD = 8
LOG2E = 1.4426950408889634
EMPTY = -1e30


def dot(a, b, dims):
    return lax.dot_general(a, b, (dims, ((), ())), preferred_element_type=jnp.float32)


def row_kernel(tiles_ref, span_ref, block_ref, line_ref, q_ref, kv_ref, out_ref, logs_ref):
    blocks, slots, width = logs_ref.shape
    per = out_ref.shape[1] // slots
    length = kv_ref.shape[1] // 2
    items = TILE // per
    scale = width ** (-0.5)
    out_ref[...] = jnp.zeros_like(out_ref)
    logs_ref[...] = jnp.zeros_like(logs_ref)

    def one_tile(t, carry):
        span = span_ref[t]
        spots = []
        for u in range(items):
            line = pl.multiple_of(line_ref[t * items + u] * per, per)
            spots.append((block_ref[t * items + u], line, line_ref[t * items + u]))
        q = jnp.concatenate([q_ref[b, pl.ds(line, per), :] for b, line, _ in spots], axis=0)
        scores = dot(kv_ref[span, :length, :], q, ((1,), (1,)))
        top = jnp.max(scores, axis=0, keepdims=True)
        weights = jnp.exp2((scores - top) * (scale * LOG2E))
        total = jnp.sum(weights, axis=0, keepdims=True)
        mixed = dot(kv_ref[span, length : 2 * length, :], weights.astype(jnp.bfloat16), ((0,), (0,)))
        mixed = (mixed * (1.0 / total)).T.astype(jnp.bfloat16)
        logs = top * scale + jnp.log(total)
        for u, (b, line, slot) in enumerate(spots):
            out_ref[b, pl.ds(line, per), :] = mixed[u * per : (u + 1) * per, :]
            logs_ref[b, pl.ds(slot, 1), 0:per] = logs[:, u * per : (u + 1) * per]
        return carry

    lax.fori_loop(0, tiles_ref[0], one_tile, 0)


def row_states(plan, q, kv, slots, per):
    blocks, _, width = q.shape
    lines = slots * per
    return pl.pallas_call(
        row_kernel,
        grid_spec=pltpu.PrefetchScalarGridSpec(
            num_scalar_prefetch=4,
            grid=(1,),
            in_specs=[
                pl.BlockSpec((blocks, lines, width), lambda i, *_: (0, 0, 0)),
                pl.BlockSpec(kv.shape, lambda i, *_: (0, 0, 0)),
            ],
            out_specs=[
                pl.BlockSpec((blocks, lines, width), lambda i, *_: (0, 0, 0)),
                pl.BlockSpec((blocks, slots, width), lambda i, *_: (0, 0, 0)),
            ],
        ),
        out_shape=[
            jax.ShapeDtypeStruct((blocks, lines, width), jnp.bfloat16),
            jax.ShapeDtypeStruct((blocks, slots, width), jnp.float32),
        ],
        compiler_params=pltpu.CompilerParams(vmem_limit_bytes=48 * 1024 * 1024),
        cost_estimate=pl.CostEstimate(
            flops=2 * q.size * kv.shape[1],
            bytes_accessed=6 * q.size + 2 * kv.size,
            transcendentals=q.size // width * kv.shape[1] // 2,
        ),
    )(*plan, q, kv)


def tile_plan(spans, count, per):
    blocks, slots = spans.shape
    items = TILE // per
    most = blocks * CAP
    rounds = -(-most // items)
    flat = spans.reshape(-1)
    names = jnp.arange(count, dtype=jnp.int32)
    equal = (flat[None, :] == names[:, None]).astype(jnp.int32)
    place = jnp.cumsum(equal, axis=1) - 1
    spot = jnp.arange(rounds * items, dtype=jnp.int32)
    hit = (place[:, None, :] == spot[None, :, None]) & (equal[:, None, :] > 0)
    lists = jnp.sum(jnp.where(hit, jnp.arange(flat.shape[0], dtype=jnp.int32), 0), axis=2)
    amount = jnp.sum(equal, axis=1)
    lists = jnp.where(spot[None, :] < amount[:, None], lists, lists[:, :1])
    tiles = jnp.minimum((amount + items - 1) // items, rounds)
    ends = jnp.cumsum(tiles)
    each = jnp.arange(count * rounds, dtype=jnp.int32)
    span = jnp.minimum(jnp.sum((ends[None, :] <= each[:, None]).astype(jnp.int32), axis=1), count - 1)
    turn = jnp.clip(each - (ends - tiles)[span], 0, rounds - 1)
    picked = lists.reshape(count * rounds, items)[span * rounds + turn].reshape(-1)
    return ends[-1:], span, picked // slots, picked % slots


def own_states(grouped, cache_keys, cache_values, fresh_keys, fresh_values, live_len):
    scaling = grouped.shape[-1] ** (-0.5)
    step_count = grouped.shape[1]
    cache_slots = cache_keys.shape[1]
    cache_scores = (
        jnp.einsum("rsngd,rtnd->rsngt", grouped, cache_keys, preferred_element_type=jnp.float32)
        * scaling
    )
    fresh_scores = (
        jnp.einsum("rsngd,rtnd->rsngt", grouped, fresh_keys, preferred_element_type=jnp.float32)
        * scaling
    )
    cache_live = jnp.arange(cache_slots, dtype=jnp.int32)[None, :] < live_len[:, None]
    cache_scores = jnp.where(cache_live[:, None, None, None, :], cache_scores, EMPTY)
    causal = (
        jnp.arange(step_count, dtype=jnp.int32)[None, :]
        <= jnp.arange(step_count, dtype=jnp.int32)[:, None]
    )
    fresh_scores = jnp.where(causal[None, :, None, None, :], fresh_scores, EMPTY)
    highest = jnp.maximum(jnp.max(cache_scores, axis=-1), jnp.max(fresh_scores, axis=-1))
    cache_w = jnp.exp(cache_scores - highest[..., None])
    fresh_w = jnp.exp(fresh_scores - highest[..., None])
    summed = jnp.sum(cache_w, axis=-1) + jnp.sum(fresh_w, axis=-1)
    product = jnp.einsum(
        "rsngt,rtnd->rsngd",
        cache_w.astype(jnp.bfloat16),
        cache_values,
        preferred_element_type=jnp.float32,
    )
    product = product + jnp.einsum(
        "rsngt,rtnd->rsngd",
        fresh_w.astype(jnp.bfloat16),
        fresh_values,
        preferred_element_type=jnp.float32,
    )
    return (product / summed[..., None], highest + jnp.log(summed))


def merge_own(parts, logs, own_part, own_log, c, per):
    requests, _, heads, width = own_part.shape
    rows = per * heads
    own_l = own_log[:, c * per : (c + 1) * per].reshape(requests, 1, rows)
    own_p = own_part[:, c * per : (c + 1) * per].reshape(requests, rows, width)
    top = jnp.maximum(jnp.max(logs, axis=1, keepdims=True), own_l)
    factors = jnp.exp(logs - top)
    own_f = jnp.exp(own_l - top)[:, 0]
    total = jnp.sum(factors, axis=1) + own_f
    merged = jnp.sum(factors[..., None] * parts.astype(jnp.float32), axis=1)
    merged = (merged + own_f[..., None] * own_p) / total[..., None]
    return merged.astype(jnp.bfloat16).reshape(requests, per, heads, width)


def local(
    queries,
    new_keys,
    new_values,
    suffix_keys,
    suffix_values,
    suffix_len,
    block_table,
    prefix_keys,
    prefix_values,
):
    requests, steps, heads, width = queries.shape
    span_count, span_len = prefix_keys.shape[:2]
    depth = block_table.shape[1]
    owners = lax.axis_size("req")
    nz = owners // NX
    in_row = NX * span_count
    column = lax.axis_index("req") % NX
    z_groups = [[z * NX + x for z in range(nz)] for x in range(NX)]
    keys = prefix_keys.reshape(span_count, span_len, width)
    values = prefix_values.reshape(span_count, span_len, width)
    per = steps // CHUNKS
    rows = per * heads

    named = block_table.reshape(-1)
    number = jnp.arange(named.shape[0], dtype=jnp.int32)
    goal = named // in_row
    before = (goal[:, None] == goal[None, :]) & (number[None, :] < number[:, None])
    rank = jnp.sum(before.astype(jnp.int32), axis=1)
    over = jnp.max((rank >= ROOM).astype(jnp.bfloat16))
    local_span = (named - column * span_count) % in_row

    def seats(low, room):
        inside = (rank >= low) & (rank < low + room)
        seat = jnp.where(inside, goal * room + rank - low, -1)
        taken = seat[None, :] == jnp.arange(nz * room, dtype=jnp.int32)[:, None]
        sender = jnp.sum(jnp.where(taken, number // depth, 0), axis=1)
        span_at = jnp.sum(jnp.where(taken, local_span + 1, 0), axis=1) - 1
        span_at = span_at.reshape(nz, room).astype(jnp.bfloat16)
        return sender, span_at, jnp.maximum(seat, 0).reshape(requests, depth)

    def along_z(array):
        return lax.all_to_all(
            array, "req", split_axis=0, concat_axis=0, tiled=True, axis_index_groups=z_groups
        )

    def send(part, sender, span_at):
        lines = sender.shape[0] // nz * part.shape[1]
        outgoing = part[sender].reshape(nz, lines, width)
        if span_at is not None:
            extra = ((0, 0), (0, PAD - 1), (0, width - span_at.shape[1]))
            outgoing = jnp.concatenate([outgoing, jnp.pad(span_at[:, None, :], extra)], axis=1)
        return along_z(outgoing)

    def packed(states, logs, note):
        lines = states.shape[1]
        logs = logs[:, :, : lines // logs.shape[1]].reshape(nz, lines)
        high = lax.reduce_precision(logs, 8, 7)
        middle = lax.reduce_precision(logs - high, 8, 7)
        logs = jnp.concatenate([high, middle, logs - high - middle], axis=1).astype(jnp.bfloat16)
        note = jnp.broadcast_to(note, (nz, PAD * width - 3 * lines))
        logs = jnp.concatenate([logs, note], axis=1).reshape(nz, PAD, width)
        return jnp.concatenate([states, logs], axis=1)

    def opened(states, slot_ids, rows):
        lines = states.shape[1] - PAD
        logs = states[:, lines:].reshape(nz, PAD * width).astype(jnp.float32)
        note = jnp.max(logs[:, -1])
        logs = logs[:, :lines] + logs[:, lines : 2 * lines] + logs[:, 2 * lines : 3 * lines]
        logs = logs.reshape(-1, rows)[slot_ids]
        parts = states[:, :lines].reshape(-1, rows, width)[slot_ids]
        return parts, logs, note

    sender, span_at, slot_ids = seats(0, ROOM)
    arrived = []
    for c in range(CHUNKS):
        part = queries[:, c * per : (c + 1) * per].reshape(requests, rows, width)
        arrived.append(send(part, sender, span_at if c == 0 else None))
    spans_named = arrived[0][:, ROOM * rows, :ROOM].astype(jnp.int32)
    plan = tile_plan(spans_named, in_row, rows)

    def along_x(array, by):
        pairs = [(z * NX + x, z * NX + (x + by) % NX) for z in range(nz) for x in range(NX)]
        return lax.ppermute(array, "req", pairs)

    note = jnp.broadcast_to(over, (span_count, 2 * PAD, width))
    mine = jnp.concatenate([keys, values, note], axis=1)
    left = along_x(mine, 1)
    right = along_x(mine, -1)
    far_keys = along_x(left[:, :span_len], 1)
    far_rest = along_x(right[:, span_len:], -1)
    lacking = jnp.maximum(over, jnp.maximum(left[0, -1, 0], right[0, -1, 0]))
    lacking = jnp.maximum(lacking, far_rest[0, -1, 0])
    both = 2 * span_len
    far = jnp.concatenate([far_keys, far_rest[:, :span_len]], axis=1)
    spans = jnp.concatenate([mine[:, :both], right[:, :both], far, left[:, :both]], axis=0)

    kv_local = new_keys.shape[2]
    grouped = queries.reshape(requests, steps, kv_local, heads // kv_local, width)
    own_part, own_log = own_states(
        grouped, suffix_keys, suffix_values, new_keys, new_values, suffix_len
    )
    own_part = own_part.reshape(requests, steps, heads, width)
    own_log = own_log.reshape(requests, steps, heads)

    results = []
    held = []
    for c in range(CHUNKS):
        states, logs = row_states(plan, arrived[c], spans, ROOM, rows)
        states = packed(states, logs, lacking)
        if c + 1 < CHUNKS:
            states, arrived[c + 1] = lax.optimization_barrier((states, arrived[c + 1]))
        states = along_z(states)
        if c > 0:
            states, results[-1] = lax.optimization_barrier((states, results[-1]))
        parts, logs, note = opened(states, slot_ids, rows)
        held.append((parts, logs))
        results.append(merge_own(parts, logs, own_part, own_log, c, per))

    def one_more_round(merged):
        room = in_row * CAP - ROOM
        all_rows = steps * heads
        sender, span_at, more_ids = seats(ROOM, room)
        incoming = send(queries.reshape(requests, all_rows, width), sender, span_at)
        named_more = incoming[:, room * all_rows, :room].astype(jnp.int32)
        plan = tile_plan(named_more, in_row, all_rows)
        states, logs = row_states(plan, incoming, spans, room, all_rows)
        states = along_z(packed(states, logs, lacking))
        more, more_logs, _ = opened(states, more_ids, all_rows)
        late = (rank >= ROOM).reshape(requests, depth, 1)
        results = []
        for c, (parts, logs) in enumerate(held):
            cut = slice(c * rows, (c + 1) * rows)
            parts = jnp.where(late[..., None], more[:, :, cut], parts)
            logs = jnp.where(late, more_logs[:, :, cut], logs)
            results.append(merge_own(parts, logs, own_part, own_log, c, per))
        return jnp.concatenate(results, axis=1)

    merged = jnp.concatenate(results, axis=1)
    merged = lax.cond(note > 0.0, one_more_round, lambda m: m, merged)
    kv_count = lax.axis_size("kv")
    merged = merged.reshape(requests // kv_count, kv_count, steps, heads * width)
    return lax.all_to_all(merged, "kv", split_axis=1, concat_axis=3, tiled=True)


def solution(mesh):
    placed = (
        P("req", None, "kv", None),
        P("req", None, "kv", None),
        P("req", None, "kv", None),
        P("req", None, "kv", None),
        P("req", None, "kv", None),
        P("req"),
        P("req", None),
        P("req", None, "kv", None),
        P("req", None, "kv", None),
    )
    return jax.shard_map(
        local, mesh=mesh, in_specs=placed, out_specs=P("req", "kv", None, None), check_vma=False
    )
```

```python
import jax
import jax.numpy as jnp
from jax import lax
from jax.experimental import pallas as pl
from jax.experimental.pallas import tpu as pltpu
from jax.sharding import PartitionSpec as P

NX = 4
CAP = 2
ROOM = 11
CHUNKS = 2
TILE = 256
PAD = 8
LOG2E = 1.4426950408889634
EMPTY = -1e30


def dot(a, b, dims):
    return lax.dot_general(a, b, (dims, ((), ())), preferred_element_type=jnp.float32)


def row_kernel(
    tiles_ref, span_ref, block_ref, line_ref,
    q_ref, mine_ref, right_ref, far_keys_ref, far_rest_ref, left_ref,
    out_ref, logs_ref, kv_ref, sems,
):
    blocks, slots, width = logs_ref.shape
    per = out_ref.shape[1] // slots
    length = kv_ref.shape[1] // 2
    items = TILE // per
    scale = width ** (-0.5)
    each = mine_ref.shape[0]
    both = 2 * length
    pieces = (
        (mine_ref.at[:, :both], kv_ref.at[:each]),
        (right_ref.at[:, :both], kv_ref.at[each : 2 * each]),
        (far_keys_ref, kv_ref.at[2 * each : 3 * each, :length]),
        (far_rest_ref.at[:, :length], kv_ref.at[2 * each : 3 * each, length:]),
        (left_ref.at[:, :both], kv_ref.at[3 * each :]),
    )
    copies = [
        pltpu.make_async_copy(piece, place, sems.at[i]) for i, (piece, place) in enumerate(pieces)
    ]
    for copy in copies:
        copy.start()
    out_ref[...] = jnp.zeros_like(out_ref)
    logs_ref[...] = jnp.zeros_like(logs_ref)
    for copy in copies:
        copy.wait()

    def one_tile(t, carry):
        span = span_ref[t]
        spots = []
        for u in range(items):
            line = pl.multiple_of(line_ref[t * items + u] * per, per)
            spots.append((block_ref[t * items + u], line, line_ref[t * items + u]))
        q = jnp.concatenate([q_ref[b, pl.ds(line, per), :] for b, line, _ in spots], axis=0)
        scores = dot(kv_ref[span, :length, :], q, ((1,), (1,)))
        top = jnp.max(scores, axis=0, keepdims=True)
        weights = jnp.exp2((scores - top) * (scale * LOG2E))
        total = jnp.sum(weights, axis=0, keepdims=True)
        mixed = dot(kv_ref[span, length : 2 * length, :], weights.astype(jnp.bfloat16), ((0,), (0,)))
        mixed = (mixed * (1.0 / total)).T.astype(jnp.bfloat16)
        logs = top * scale + jnp.log(total)
        for u, (b, line, slot) in enumerate(spots):
            out_ref[b, pl.ds(line, per), :] = mixed[u * per : (u + 1) * per, :]
            logs_ref[b, pl.ds(slot, 1), 0:per] = logs[:, u * per : (u + 1) * per]
        return carry

    lax.fori_loop(0, tiles_ref[0], one_tile, 0)


def row_states(plan, q, spans, slots, per):
    blocks, _, width = q.shape
    lines = slots * per
    each, length = spans[2].shape[:2]
    return pl.pallas_call(
        row_kernel,
        grid_spec=pltpu.PrefetchScalarGridSpec(
            num_scalar_prefetch=4,
            grid=(1,),
            in_specs=[
                pl.BlockSpec((blocks, lines, width), lambda i, *_: (0, 0, 0)),
            ]
            + [pl.BlockSpec(memory_space=pl.ANY)] * len(spans),
            out_specs=[
                pl.BlockSpec((blocks, lines, width), lambda i, *_: (0, 0, 0)),
                pl.BlockSpec((blocks, slots, width), lambda i, *_: (0, 0, 0)),
            ],
            scratch_shapes=[
                pltpu.VMEM((NX * each, 2 * length, width), jnp.bfloat16),
                pltpu.SemaphoreType.DMA((len(spans),)),
            ],
        ),
        out_shape=[
            jax.ShapeDtypeStruct((blocks, lines, width), jnp.bfloat16),
            jax.ShapeDtypeStruct((blocks, slots, width), jnp.float32),
        ],
        compiler_params=pltpu.CompilerParams(vmem_limit_bytes=48 * 1024 * 1024),
        cost_estimate=pl.CostEstimate(
            flops=q.size, bytes_accessed=4 * q.size, transcendentals=0
        ),
    )(*plan, q, *spans)


def tile_plan(spans, count, per):
    blocks, slots = spans.shape
    items = TILE // per
    most = blocks * CAP
    rounds = -(-most // items)
    flat = spans.reshape(-1)
    names = jnp.arange(count, dtype=jnp.int32)
    equal = (flat[None, :] == names[:, None]).astype(jnp.int32)
    place = jnp.cumsum(equal, axis=1) - 1
    spot = jnp.arange(rounds * items, dtype=jnp.int32)
    hit = (place[:, None, :] == spot[None, :, None]) & (equal[:, None, :] > 0)
    lists = jnp.sum(jnp.where(hit, jnp.arange(flat.shape[0], dtype=jnp.int32), 0), axis=2)
    amount = jnp.sum(equal, axis=1)
    lists = jnp.where(spot[None, :] < amount[:, None], lists, lists[:, :1])
    tiles = jnp.minimum((amount + items - 1) // items, rounds)
    ends = jnp.cumsum(tiles)
    each = jnp.arange(count * rounds, dtype=jnp.int32)
    span = jnp.minimum(jnp.sum((ends[None, :] <= each[:, None]).astype(jnp.int32), axis=1), count - 1)
    turn = jnp.clip(each - (ends - tiles)[span], 0, rounds - 1)
    picked = lists.reshape(count * rounds, items)[span * rounds + turn].reshape(-1)
    return ends[-1:], span, picked // slots, picked % slots


def own_states(grouped, cache_keys, cache_values, fresh_keys, fresh_values, live_len):
    scaling = grouped.shape[-1] ** (-0.5)
    step_count = grouped.shape[1]
    cache_slots = cache_keys.shape[1]
    cache_scores = (
        jnp.einsum("rsngd,rtnd->rsngt", grouped, cache_keys, preferred_element_type=jnp.float32)
        * scaling
    )
    fresh_scores = (
        jnp.einsum("rsngd,rtnd->rsngt", grouped, fresh_keys, preferred_element_type=jnp.float32)
        * scaling
    )
    cache_live = jnp.arange(cache_slots, dtype=jnp.int32)[None, :] < live_len[:, None]
    cache_scores = jnp.where(cache_live[:, None, None, None, :], cache_scores, EMPTY)
    causal = (
        jnp.arange(step_count, dtype=jnp.int32)[None, :]
        <= jnp.arange(step_count, dtype=jnp.int32)[:, None]
    )
    fresh_scores = jnp.where(causal[None, :, None, None, :], fresh_scores, EMPTY)
    highest = jnp.maximum(jnp.max(cache_scores, axis=-1), jnp.max(fresh_scores, axis=-1))
    cache_w = jnp.exp(cache_scores - highest[..., None])
    fresh_w = jnp.exp(fresh_scores - highest[..., None])
    summed = jnp.sum(cache_w, axis=-1) + jnp.sum(fresh_w, axis=-1)
    product = jnp.einsum(
        "rsngt,rtnd->rsngd",
        cache_w.astype(jnp.bfloat16),
        cache_values,
        preferred_element_type=jnp.float32,
    )
    product = product + jnp.einsum(
        "rsngt,rtnd->rsngd",
        fresh_w.astype(jnp.bfloat16),
        fresh_values,
        preferred_element_type=jnp.float32,
    )
    return (product / summed[..., None], highest + jnp.log(summed))


def merge_own(parts, logs, own_part, own_log, c, per):
    requests, _, heads, width = own_part.shape
    rows = per * heads
    own_l = own_log[:, c * per : (c + 1) * per].reshape(requests, 1, rows)
    own_p = own_part[:, c * per : (c + 1) * per].reshape(requests, rows, width)
    top = jnp.maximum(jnp.max(logs, axis=1, keepdims=True), own_l)
    factors = jnp.exp(logs - top)
    own_f = jnp.exp(own_l - top)[:, 0]
    total = jnp.sum(factors, axis=1) + own_f
    merged = jnp.sum(factors[..., None] * parts.astype(jnp.float32), axis=1)
    merged = (merged + own_f[..., None] * own_p) / total[..., None]
    return merged.astype(jnp.bfloat16).reshape(requests, per, heads, width)


def local(
    queries,
    new_keys,
    new_values,
    suffix_keys,
    suffix_values,
    suffix_len,
    block_table,
    prefix_keys,
    prefix_values,
):
    requests, steps, heads, width = queries.shape
    span_count, span_len = prefix_keys.shape[:2]
    depth = block_table.shape[1]
    owners = lax.axis_size("req")
    nz = owners // NX
    in_row = NX * span_count
    column = lax.axis_index("req") % NX
    z_groups = [[z * NX + x for z in range(nz)] for x in range(NX)]
    keys = prefix_keys.reshape(span_count, span_len, width)
    values = prefix_values.reshape(span_count, span_len, width)
    per = steps // CHUNKS
    rows = per * heads

    named = block_table.reshape(-1)
    number = jnp.arange(named.shape[0], dtype=jnp.int32)
    goal = named // in_row
    before = (goal[:, None] == goal[None, :]) & (number[None, :] < number[:, None])
    rank = jnp.sum(before.astype(jnp.int32), axis=1)
    over = jnp.max((rank >= ROOM).astype(jnp.bfloat16))
    local_span = (named - column * span_count) % in_row

    def seats(low, room):
        inside = (rank >= low) & (rank < low + room)
        seat = jnp.where(inside, goal * room + rank - low, -1)
        taken = seat[None, :] == jnp.arange(nz * room, dtype=jnp.int32)[:, None]
        sender = jnp.sum(jnp.where(taken, number // depth, 0), axis=1)
        span_at = jnp.sum(jnp.where(taken, local_span + 1, 0), axis=1) - 1
        span_at = span_at.reshape(nz, room).astype(jnp.bfloat16)
        return sender, span_at, jnp.maximum(seat, 0).reshape(requests, depth)

    def along_z(array):
        return lax.all_to_all(
            array, "req", split_axis=0, concat_axis=0, tiled=True, axis_index_groups=z_groups
        )

    def send(part, sender, span_at):
        lines = sender.shape[0] // nz * part.shape[1]
        outgoing = part[sender].reshape(nz, lines, width)
        if span_at is not None:
            extra = ((0, 0), (0, PAD - 1), (0, width - span_at.shape[1]))
            outgoing = jnp.concatenate([outgoing, jnp.pad(span_at[:, None, :], extra)], axis=1)
        return along_z(outgoing)

    def packed(states, logs, note):
        lines = states.shape[1]
        logs = logs[:, :, : lines // logs.shape[1]].reshape(nz, lines)
        high = lax.reduce_precision(logs, 8, 7)
        middle = lax.reduce_precision(logs - high, 8, 7)
        logs = jnp.concatenate([high, middle, logs - high - middle], axis=1).astype(jnp.bfloat16)
        note = jnp.broadcast_to(note, (nz, PAD * width - 3 * lines))
        logs = jnp.concatenate([logs, note], axis=1).reshape(nz, PAD, width)
        return jnp.concatenate([states, logs], axis=1)

    def opened(states, slot_ids, rows):
        lines = states.shape[1] - PAD
        logs = states[:, lines:].reshape(nz, PAD * width).astype(jnp.float32)
        note = jnp.max(logs[:, -1])
        logs = logs[:, :lines] + logs[:, lines : 2 * lines] + logs[:, 2 * lines : 3 * lines]
        logs = logs.reshape(-1, rows)[slot_ids]
        parts = states[:, :lines].reshape(-1, rows, width)[slot_ids]
        return parts, logs, note

    sender, span_at, slot_ids = seats(0, ROOM)
    arrived = []
    for c in range(CHUNKS):
        part = queries[:, c * per : (c + 1) * per].reshape(requests, rows, width)
        arrived.append(send(part, sender, span_at if c == 0 else None))
    spans_named = arrived[0][:, ROOM * rows, :ROOM].astype(jnp.int32)
    plan = tile_plan(spans_named, in_row, rows)

    def along_x(array, by):
        pairs = [(z * NX + x, z * NX + (x + by) % NX) for z in range(nz) for x in range(NX)]
        return lax.ppermute(array, "req", pairs)

    note = jnp.broadcast_to(over, (span_count, 2 * PAD, width))
    mine = jnp.concatenate([keys, values, note], axis=1)
    left = along_x(mine, 1)
    right = along_x(mine, -1)
    far_keys = along_x(left[:, :span_len], 1)
    far_rest = along_x(right[:, span_len:], -1)
    lacking = jnp.maximum(over, jnp.maximum(left[0, -1, 0], right[0, -1, 0]))
    lacking = jnp.maximum(lacking, far_rest[0, -1, 0])
    spans = (mine, right, far_keys, far_rest, left)

    kv_local = new_keys.shape[2]
    grouped = queries.reshape(requests, steps, kv_local, heads // kv_local, width)
    own_part, own_log = own_states(
        grouped, suffix_keys, suffix_values, new_keys, new_values, suffix_len
    )
    own_part = own_part.reshape(requests, steps, heads, width)
    own_log = own_log.reshape(requests, steps, heads)

    results = []
    held = []
    for c in range(CHUNKS):
        states, logs = row_states(plan, arrived[c], spans, ROOM, rows)
        states = packed(states, logs, lacking)
        if c + 1 < CHUNKS:
            states, arrived[c + 1] = lax.optimization_barrier((states, arrived[c + 1]))
        states = along_z(states)
        if c > 0:
            states, results[-1] = lax.optimization_barrier((states, results[-1]))
        parts, logs, note = opened(states, slot_ids, rows)
        held.append((parts, logs))
        results.append(merge_own(parts, logs, own_part, own_log, c, per))

    def one_more_round(merged):
        room = in_row * CAP - ROOM
        all_rows = steps * heads
        sender, span_at, more_ids = seats(ROOM, room)
        incoming = send(queries.reshape(requests, all_rows, width), sender, span_at)
        named_more = incoming[:, room * all_rows, :room].astype(jnp.int32)
        plan = tile_plan(named_more, in_row, all_rows)
        states, logs = row_states(plan, incoming, spans, room, all_rows)
        states = along_z(packed(states, logs, lacking))
        more, more_logs, _ = opened(states, more_ids, all_rows)
        late = (rank >= ROOM).reshape(requests, depth, 1)
        results = []
        for c, (parts, logs) in enumerate(held):
            cut = slice(c * rows, (c + 1) * rows)
            parts = jnp.where(late[..., None], more[:, :, cut], parts)
            logs = jnp.where(late, more_logs[:, :, cut], logs)
            results.append(merge_own(parts, logs, own_part, own_log, c, per))
        return jnp.concatenate(results, axis=1)

    merged = jnp.concatenate(results, axis=1)
    merged = lax.cond(note > 0.0, one_more_round, lambda m: m, merged)
    kv_count = lax.axis_size("kv")
    merged = merged.reshape(requests // kv_count, kv_count, steps, heads * width)
    return lax.all_to_all(merged, "kv", split_axis=1, concat_axis=3, tiled=True)


def solution(mesh):
    placed = (
        P("req", None, "kv", None),
        P("req", None, "kv", None),
        P("req", None, "kv", None),
        P("req", None, "kv", None),
        P("req", None, "kv", None),
        P("req"),
        P("req", None),
        P("req", None, "kv", None),
        P("req", None, "kv", None),
    )
    return jax.shard_map(
        local, mesh=mesh, in_specs=placed, out_specs=P("req", "kv", None, None), check_vma=False
    )
```

```python
import jax
import jax.numpy as jnp
from jax import lax
from jax.experimental import pallas as pl
from jax.experimental.pallas import tpu as pltpu
from jax.sharding import PartitionSpec as P

NX = 4
CAP = 2
ROOM = 11
CHUNKS = 2
TILE = 256
PAD = 8
LOG2E = 1.4426950408889634
EMPTY = -1e30


def dot(a, b, dims):
    return lax.dot_general(a, b, (dims, ((), ())), preferred_element_type=jnp.float32)


def row_kernel(
    shift, stride, ids_ref, q_ref, mine_ref, right_ref, far_keys_ref, far_rest_ref, left_ref,
    out_ref, logs_ref, kv_ref, sems, count_ref, block_ref, slot_ref, span_ref, start_ref,
):
    blocks, slots, width = logs_ref.shape
    per = out_ref.shape[1] // slots
    spans, both = kv_ref.shape[:2]
    length = both // 2
    items = TILE // per
    most = blocks * CAP
    scale = width ** (-0.5)
    each = mine_ref.shape[0]
    pieces = (
        (mine_ref.at[:, :both], kv_ref.at[:each]),
        (right_ref.at[:, :both], kv_ref.at[each : 2 * each]),
        (far_keys_ref, kv_ref.at[2 * each : 3 * each, :length]),
        (far_rest_ref.at[:, :length], kv_ref.at[2 * each : 3 * each, length:]),
        (left_ref.at[:, :both], kv_ref.at[3 * each :]),
    )
    copies = [
        pltpu.make_async_copy(piece, place, sems.at[i]) for i, (piece, place) in enumerate(pieces)
    ]
    for copy in copies:
        copy.start()
    out_ref[...] = jnp.zeros_like(out_ref)
    logs_ref[...] = jnp.zeros_like(logs_ref)

    for s in range(spans + 1):
        count_ref[s] = 0

    def one_block(b, carry):
        for c in range(slots):
            name = ids_ref[b * slots + c]
            name = jnp.where(name < 0, spans, name)
            place = jnp.minimum(count_ref[name], most - 1)
            block_ref[name * most + place] = b
            slot_ref[name * most + place] = c
            count_ref[name] = place + 1
        return carry

    lax.fori_loop(0, blocks, one_block, 0)
    tiles = jnp.int32(0)
    for s in range(spans):
        for t in range(-(-most // items)):
            span_ref[tiles] = s
            start_ref[tiles] = t * items
            tiles = tiles + jnp.where(count_ref[s] > t * items, 1, 0)
    for copy in copies:
        copy.wait()

    def spots_of(tile):
        span = span_ref[tile]
        start = start_ref[tile]
        last = count_ref[span] - 1
        spots = []
        for u in range(items):
            at = span * most + jnp.minimum(start + u, last)
            spots.append((block_ref[at], slot_ref[at]))
        return span, spots

    def two_tiles(t, carry):
        work = [spots_of(2 * t), spots_of(jnp.minimum(2 * t + 1, tiles - 1))]
        scores = []
        for span, spots in work:
            q = jnp.concatenate(
                [
                    q_ref[b, pl.ds(pl.multiple_of(c * stride + shift, 16), per), :]
                    for b, c in spots
                ],
                axis=0,
            )
            scores.append(dot(kv_ref[span, :length, :], q, ((1,), (1,))))
        done = []
        for (span, spots), score in zip(work, scores):
            top = jnp.max(score, axis=0, keepdims=True)
            weights = jnp.exp2((score - top) * (scale * LOG2E))
            total = jnp.sum(weights, axis=0, keepdims=True)
            mixed = dot(kv_ref[span, length:, :], weights.astype(jnp.bfloat16), ((0,), (0,)))
            done.append((mixed * (1.0 / total), top * scale + jnp.log(total)))
        for (span, spots), (mixed, logs) in zip(work, done):
            mixed = mixed.T.astype(jnp.bfloat16)
            for u, (b, c) in enumerate(spots):
                line = pl.multiple_of(c * per, 16)
                out_ref[b, pl.ds(line, per), :] = mixed[u * per : (u + 1) * per, :]
                logs_ref[b, pl.ds(c, 1), 0:per] = logs[:, u * per : (u + 1) * per]
        return carry

    lax.fori_loop(0, (tiles + 1) // 2, two_tiles, 0)


def row_states(ids, q, spans, slots, shift, per, stride):
    blocks, _, width = q.shape
    lines = slots * per
    each, length = spans[2].shape[:2]
    count = NX * each
    most = blocks * CAP
    tiles = count * -(-most * per // TILE) + 1
    return pl.pallas_call(
        lambda *refs: row_kernel(shift, stride, *refs),
        grid_spec=pltpu.PrefetchScalarGridSpec(
            num_scalar_prefetch=1,
            grid=(1,),
            in_specs=[pl.BlockSpec((blocks, slots * stride, width), lambda i, *_: (0, 0, 0))]
            + [pl.BlockSpec(memory_space=pl.ANY)] * len(spans),
            out_specs=[
                pl.BlockSpec((blocks, lines, width), lambda i, *_: (0, 0, 0)),
                pl.BlockSpec((blocks, slots, width), lambda i, *_: (0, 0, 0)),
            ],
            scratch_shapes=[
                pltpu.VMEM((count, 2 * length, width), jnp.bfloat16),
                pltpu.SemaphoreType.DMA((len(spans),)),
                pltpu.SMEM((count + 1,), jnp.int32),
                pltpu.SMEM(((count + 1) * most,), jnp.int32),
                pltpu.SMEM(((count + 1) * most,), jnp.int32),
                pltpu.SMEM((tiles,), jnp.int32),
                pltpu.SMEM((tiles,), jnp.int32),
            ],
        ),
        out_shape=[
            jax.ShapeDtypeStruct((blocks, lines, width), jnp.bfloat16),
            jax.ShapeDtypeStruct((blocks, slots, width), jnp.float32),
        ],
        compiler_params=pltpu.CompilerParams(vmem_limit_bytes=24 * 1024 * 1024),
        cost_estimate=pl.CostEstimate(
            flops=q.size, bytes_accessed=4 * q.size, transcendentals=0
        ),
    )(ids, q, *spans)


def own_states(grouped, cache_keys, cache_values, fresh_keys, fresh_values, live_len):
    scaling = grouped.shape[-1] ** (-0.5)
    step_count = grouped.shape[1]
    cache_slots = cache_keys.shape[1]
    cache_scores = (
        jnp.einsum("rsngd,rtnd->rsngt", grouped, cache_keys, preferred_element_type=jnp.float32)
        * scaling
    )
    fresh_scores = (
        jnp.einsum("rsngd,rtnd->rsngt", grouped, fresh_keys, preferred_element_type=jnp.float32)
        * scaling
    )
    cache_live = jnp.arange(cache_slots, dtype=jnp.int32)[None, :] < live_len[:, None]
    cache_scores = jnp.where(cache_live[:, None, None, None, :], cache_scores, EMPTY)
    causal = (
        jnp.arange(step_count, dtype=jnp.int32)[None, :]
        <= jnp.arange(step_count, dtype=jnp.int32)[:, None]
    )
    fresh_scores = jnp.where(causal[None, :, None, None, :], fresh_scores, EMPTY)
    highest = jnp.maximum(jnp.max(cache_scores, axis=-1), jnp.max(fresh_scores, axis=-1))
    cache_w = jnp.exp(cache_scores - highest[..., None])
    fresh_w = jnp.exp(fresh_scores - highest[..., None])
    summed = jnp.sum(cache_w, axis=-1) + jnp.sum(fresh_w, axis=-1)
    product = jnp.einsum(
        "rsngt,rtnd->rsngd",
        cache_w.astype(jnp.bfloat16),
        cache_values,
        preferred_element_type=jnp.float32,
    )
    product = product + jnp.einsum(
        "rsngt,rtnd->rsngd",
        fresh_w.astype(jnp.bfloat16),
        fresh_values,
        preferred_element_type=jnp.float32,
    )
    return (product / summed[..., None], highest + jnp.log(summed))


def merge_own(parts, logs, own_part, own_log, c, per):
    requests, _, heads, width = own_part.shape
    rows = per * heads
    own_l = own_log[:, c * per : (c + 1) * per].reshape(requests, 1, rows)
    own_p = own_part[:, c * per : (c + 1) * per].reshape(requests, rows, width)
    top = jnp.maximum(jnp.max(logs, axis=1, keepdims=True), own_l)
    factors = jnp.exp(logs - top)
    own_f = jnp.exp(own_l - top)[:, 0]
    total = jnp.sum(factors, axis=1) + own_f
    merged = jnp.sum(factors[..., None] * parts.astype(jnp.float32), axis=1)
    merged = (merged + own_f[..., None] * own_p) / total[..., None]
    return merged.astype(jnp.bfloat16).reshape(requests, per, heads, width)


def local(
    queries,
    new_keys,
    new_values,
    suffix_keys,
    suffix_values,
    suffix_len,
    block_table,
    prefix_keys,
    prefix_values,
):
    requests, steps, heads, width = queries.shape
    span_count, span_len = prefix_keys.shape[:2]
    depth = block_table.shape[1]
    owners = lax.axis_size("req")
    nz = owners // NX
    in_row = NX * span_count
    column = lax.axis_index("req") % NX
    z_groups = [[z * NX + x for z in range(nz)] for x in range(NX)]
    keys = prefix_keys.reshape(span_count, span_len, width)
    values = prefix_values.reshape(span_count, span_len, width)
    per = steps // CHUNKS
    rows = per * heads

    named = block_table.reshape(-1)
    number = jnp.arange(named.shape[0], dtype=jnp.int32)
    goal = named // in_row
    before = (goal[:, None] == goal[None, :]) & (number[None, :] < number[:, None])
    rank = jnp.sum(before.astype(jnp.int32), axis=1)
    over = jnp.max((rank >= ROOM).astype(jnp.bfloat16))
    local_span = (named - column * span_count) % in_row

    def seats(low, room):
        inside = (rank >= low) & (rank < low + room)
        seat = jnp.where(inside, goal * room + rank - low, -1)
        taken = seat[None, :] == jnp.arange(nz * room, dtype=jnp.int32)[:, None]
        sender = jnp.sum(jnp.where(taken, number // depth, 0), axis=1)
        span_at = jnp.sum(jnp.where(taken, local_span + 1, 0), axis=1) - 1
        span_at = span_at.reshape(nz, room).astype(jnp.bfloat16)
        return sender, span_at, jnp.maximum(seat, 0).reshape(requests, depth)

    def along_z(array):
        return lax.all_to_all(
            array, "req", split_axis=0, concat_axis=0, tiled=True, axis_index_groups=z_groups
        )

    def send(part, sender, span_at):
        room = span_at.shape[1]
        lines = room * part.shape[1]
        outgoing = part[sender].reshape(nz, lines, width)
        extra = ((0, 0), (0, PAD - 1), (0, width - room))
        outgoing = jnp.concatenate([outgoing, jnp.pad(span_at[:, None, :], extra)], axis=1)
        incoming = along_z(outgoing)
        return incoming, incoming[:, lines, :room].astype(jnp.int32).reshape(-1)

    def packed(states, logs, note):
        lines = states.shape[1]
        logs = logs[:, :, : lines // logs.shape[1]].reshape(nz, lines)
        high = lax.reduce_precision(logs, 8, 7)
        middle = lax.reduce_precision(logs - high, 8, 7)
        logs = jnp.concatenate([high, middle, logs - high - middle], axis=1).astype(jnp.bfloat16)
        note = jnp.broadcast_to(note, (nz, PAD * width - 3 * lines))
        logs = jnp.concatenate([logs, note], axis=1).reshape(nz, PAD, width)
        return jnp.concatenate([states, logs], axis=1)

    def opened(states, slot_ids, rows):
        lines = states.shape[1] - PAD
        logs = states[:, lines:].reshape(nz, PAD * width).astype(jnp.float32)
        note = jnp.max(logs[:, -1])
        logs = logs[:, :lines] + logs[:, lines : 2 * lines] + logs[:, 2 * lines : 3 * lines]
        logs = logs.reshape(-1, rows)[slot_ids]
        parts = states[:, :lines].reshape(-1, rows, width)[slot_ids]
        return parts, logs, note

    sender, span_at, slot_ids = seats(0, ROOM)
    all_rows = steps * heads
    everything = queries.reshape(requests, all_rows, width)
    arrived, ids = send(everything, sender, span_at)

    def along_x(array, by):
        pairs = [(z * NX + x, z * NX + (x + by) % NX) for z in range(nz) for x in range(NX)]
        return lax.ppermute(array, "req", pairs)

    note = jnp.broadcast_to(over, (span_count, 2 * PAD, width))
    mine = jnp.concatenate([keys, values, note], axis=1)
    left = along_x(mine, 1)
    right = along_x(mine, -1)
    far_keys = along_x(left[:, :span_len], 1)
    far_rest = along_x(right[:, span_len:], -1)
    lacking = jnp.maximum(over, jnp.maximum(left[0, -1, 0], right[0, -1, 0]))
    lacking = jnp.maximum(lacking, far_rest[0, -1, 0])
    spans = (mine, right, far_keys, far_rest, left)

    kv_local = new_keys.shape[2]
    grouped = queries.reshape(requests, steps, kv_local, heads // kv_local, width)
    own_part, own_log = own_states(
        grouped, suffix_keys, suffix_values, new_keys, new_values, suffix_len
    )
    own_part = own_part.reshape(requests, steps, heads, width)
    own_log = own_log.reshape(requests, steps, heads)

    results = []
    held = []
    for c in range(CHUNKS):
        states, logs = row_states(ids, arrived, spans, ROOM, c * rows, rows, all_rows)
        states = packed(states, logs, lacking)
        states = along_z(states)
        if c > 0:
            states, results[-1] = lax.optimization_barrier((states, results[-1]))
        parts, logs, note = opened(states, slot_ids, rows)
        held.append((parts, logs))
        results.append(merge_own(parts, logs, own_part, own_log, c, per))

    def one_more_round(merged):
        room = in_row * CAP - ROOM
        sender, span_at, more_ids = seats(ROOM, room)
        incoming, ids = send(everything, sender, span_at)
        states, logs = row_states(ids, incoming, spans, room, 0, all_rows, all_rows)
        states = along_z(packed(states, logs, lacking))
        more, more_logs, _ = opened(states, more_ids, all_rows)
        late = (rank >= ROOM).reshape(requests, depth, 1)
        results = []
        for c, (parts, logs) in enumerate(held):
            cut = slice(c * rows, (c + 1) * rows)
            parts = jnp.where(late[..., None], more[:, :, cut], parts)
            logs = jnp.where(late, more_logs[:, :, cut], logs)
            results.append(merge_own(parts, logs, own_part, own_log, c, per))
        return jnp.concatenate(results, axis=1)

    merged = jnp.concatenate(results, axis=1)
    merged = lax.cond(note > 0.0, one_more_round, lambda m: m, merged)
    kv_count = lax.axis_size("kv")
    merged = merged.reshape(requests // kv_count, kv_count, steps, heads * width)
    return lax.all_to_all(merged, "kv", split_axis=1, concat_axis=3, tiled=True)


def solution(mesh):
    placed = (
        P("req", None, "kv", None),
        P("req", None, "kv", None),
        P("req", None, "kv", None),
        P("req", None, "kv", None),
        P("req", None, "kv", None),
        P("req"),
        P("req", None),
        P("req", None, "kv", None),
        P("req", None, "kv", None),
    )
    return jax.shard_map(
        local, mesh=mesh, in_specs=placed, out_specs=P("req", "kv", None, None), check_vma=False
    )
```

```python
import jax
import jax.numpy as jnp
from jax import lax
from jax.experimental import pallas as pl
from jax.experimental.pallas import tpu as pltpu
from jax.sharding import PartitionSpec as P

NX = 4
CAP = 2
ROOM = 11
CHUNKS = 2
TILE = 256
PAD = 8
LOG2E = 1.4426950408889634
EMPTY = -1e30


def dot(a, b, dims):
    return lax.dot_general(a, b, (dims, ((), ())), preferred_element_type=jnp.float32)


def row_kernel(
    shift, stride, ids_ref, q_ref, mine_ref, right_ref, far_keys_ref, far_rest_ref, left_ref,
    out_ref, logs_ref, kv_ref, sems, count_ref, block_ref, slot_ref, span_ref, start_ref,
):
    blocks, slots, width = logs_ref.shape
    per = out_ref.shape[1] // slots
    spans, both = kv_ref.shape[:2]
    length = both // 2
    items = TILE // per
    most = blocks * CAP
    scale = width ** (-0.5)
    each = mine_ref.shape[0]
    pieces = (
        (mine_ref.at[:, :both], kv_ref.at[:each]),
        (right_ref.at[:, :both], kv_ref.at[each : 2 * each]),
        (far_keys_ref, kv_ref.at[2 * each : 3 * each, :length]),
        (far_rest_ref.at[:, :length], kv_ref.at[2 * each : 3 * each, length:]),
        (left_ref.at[:, :both], kv_ref.at[3 * each :]),
    )
    copies = [
        pltpu.make_async_copy(piece, place, sems.at[i]) for i, (piece, place) in enumerate(pieces)
    ]
    for copy in copies:
        copy.start()
    out_ref[...] = jnp.zeros_like(out_ref)
    logs_ref[...] = jnp.zeros_like(logs_ref)

    for s in range(spans + 1):
        count_ref[s] = 0

    def one_block(b, carry):
        for c in range(slots):
            name = ids_ref[b * slots + c]
            name = jnp.where(name < 0, spans, name)
            place = jnp.minimum(count_ref[name], most - 1)
            block_ref[name * most + place] = b
            slot_ref[name * most + place] = c
            count_ref[name] = place + 1
        return carry

    lax.fori_loop(0, blocks, one_block, 0)
    tiles = jnp.int32(0)
    for s in range(spans):
        for t in range(-(-most // items)):
            span_ref[tiles] = s
            start_ref[tiles] = t * items
            tiles = tiles + jnp.where(count_ref[s] > t * items, 1, 0)
    for copy in copies:
        copy.wait()

    def spots_of(tile):
        span = span_ref[tile]
        start = start_ref[tile]
        last = count_ref[span] - 1
        spots = []
        for u in range(items):
            at = span * most + jnp.minimum(start + u, last)
            spots.append((block_ref[at], slot_ref[at]))
        return span, spots

    def two_tiles(t, carry):
        work = [spots_of(2 * t), spots_of(jnp.minimum(2 * t + 1, tiles - 1))]
        scores = []
        for span, spots in work:
            q = jnp.concatenate(
                [
                    q_ref[b, pl.ds(pl.multiple_of(c * stride + shift, 16), per), :]
                    for b, c in spots
                ],
                axis=0,
            )
            scores.append(dot(kv_ref[span, :length, :], q, ((1,), (1,))))
        done = []
        for (span, spots), score in zip(work, scores):
            top = jnp.max(score, axis=0, keepdims=True)
            weights = jnp.exp2((score - top) * (scale * LOG2E))
            total = jnp.sum(weights, axis=0, keepdims=True)
            mixed = dot(kv_ref[span, length:, :], weights.astype(jnp.bfloat16), ((0,), (0,)))
            done.append((mixed * (1.0 / total), top * scale + jnp.log(total)))
        for (span, spots), (mixed, logs) in zip(work, done):
            mixed = mixed.T.astype(jnp.bfloat16)
            for u, (b, c) in enumerate(spots):
                line = pl.multiple_of(c * per, 16)
                out_ref[b, pl.ds(line, per), :] = mixed[u * per : (u + 1) * per, :]
                logs_ref[b, pl.ds(c, 1), 0:per] = logs[:, u * per : (u + 1) * per]
        return carry

    lax.fori_loop(0, (tiles + 1) // 2, two_tiles, 0)


def row_states(ids, q, spans, slots, shift, per, stride):
    blocks, _, width = q.shape
    lines = slots * per
    each, length = spans[2].shape[:2]
    count = NX * each
    most = blocks * CAP
    tiles = count * -(-most * per // TILE) + 1
    return pl.pallas_call(
        lambda *refs: row_kernel(shift, stride, *refs),
        grid_spec=pltpu.PrefetchScalarGridSpec(
            num_scalar_prefetch=1,
            grid=(1,),
            in_specs=[pl.BlockSpec((blocks, slots * stride, width), lambda i, *_: (0, 0, 0))]
            + [pl.BlockSpec(memory_space=pl.ANY)] * len(spans),
            out_specs=[
                pl.BlockSpec((blocks, lines, width), lambda i, *_: (0, 0, 0)),
                pl.BlockSpec((blocks, slots, width), lambda i, *_: (0, 0, 0)),
            ],
            scratch_shapes=[
                pltpu.VMEM((count, 2 * length, width), jnp.bfloat16),
                pltpu.SemaphoreType.DMA((len(spans),)),
                pltpu.SMEM((count + 1,), jnp.int32),
                pltpu.SMEM(((count + 1) * most,), jnp.int32),
                pltpu.SMEM(((count + 1) * most,), jnp.int32),
                pltpu.SMEM((tiles,), jnp.int32),
                pltpu.SMEM((tiles,), jnp.int32),
            ],
        ),
        out_shape=[
            jax.ShapeDtypeStruct((blocks, lines, width), jnp.bfloat16),
            jax.ShapeDtypeStruct((blocks, slots, width), jnp.float32),
        ],
        compiler_params=pltpu.CompilerParams(vmem_limit_bytes=24 * 1024 * 1024),
        cost_estimate=pl.CostEstimate(
            flops=q.size, bytes_accessed=4 * q.size, transcendentals=0
        ),
    )(ids, q, *spans)


def own_states(grouped, cache_keys, cache_values, fresh_keys, fresh_values, live_len):
    scaling = grouped.shape[-1] ** (-0.5)
    step_count = grouped.shape[1]
    cache_slots = cache_keys.shape[1]
    cache_scores = (
        jnp.einsum("rsngd,rtnd->rsngt", grouped, cache_keys, preferred_element_type=jnp.float32)
        * scaling
    )
    fresh_scores = (
        jnp.einsum("rsngd,rtnd->rsngt", grouped, fresh_keys, preferred_element_type=jnp.float32)
        * scaling
    )
    cache_live = jnp.arange(cache_slots, dtype=jnp.int32)[None, :] < live_len[:, None]
    cache_scores = jnp.where(cache_live[:, None, None, None, :], cache_scores, EMPTY)
    causal = (
        jnp.arange(step_count, dtype=jnp.int32)[None, :]
        <= jnp.arange(step_count, dtype=jnp.int32)[:, None]
    )
    fresh_scores = jnp.where(causal[None, :, None, None, :], fresh_scores, EMPTY)
    highest = jnp.maximum(jnp.max(cache_scores, axis=-1), jnp.max(fresh_scores, axis=-1))
    cache_w = jnp.exp(cache_scores - highest[..., None])
    fresh_w = jnp.exp(fresh_scores - highest[..., None])
    summed = jnp.sum(cache_w, axis=-1) + jnp.sum(fresh_w, axis=-1)
    product = jnp.einsum(
        "rsngt,rtnd->rsngd",
        cache_w.astype(jnp.bfloat16),
        cache_values,
        preferred_element_type=jnp.float32,
    )
    product = product + jnp.einsum(
        "rsngt,rtnd->rsngd",
        fresh_w.astype(jnp.bfloat16),
        fresh_values,
        preferred_element_type=jnp.float32,
    )
    return (product / summed[..., None], highest + jnp.log(summed))


def merge_own(parts, logs, own_part, own_log, c, per):
    requests, _, heads, width = own_part.shape
    rows = per * heads
    own_l = own_log[:, c * per : (c + 1) * per].reshape(requests, 1, rows)
    own_p = own_part[:, c * per : (c + 1) * per].reshape(requests, rows, width)
    top = jnp.maximum(jnp.max(logs, axis=1, keepdims=True), own_l)
    factors = jnp.exp(logs - top)
    own_f = jnp.exp(own_l - top)[:, 0]
    total = jnp.sum(factors, axis=1) + own_f
    merged = jnp.sum(factors[..., None] * parts.astype(jnp.float32), axis=1)
    merged = (merged + own_f[..., None] * own_p) / total[..., None]
    return merged.astype(jnp.bfloat16).reshape(requests, per, heads, width)


def local(
    queries,
    new_keys,
    new_values,
    suffix_keys,
    suffix_values,
    suffix_len,
    block_table,
    prefix_keys,
    prefix_values,
):
    requests, steps, heads, width = queries.shape
    span_count, span_len = prefix_keys.shape[:2]
    depth = block_table.shape[1]
    owners = lax.axis_size("req")
    nz = owners // NX
    in_row = NX * span_count
    column = lax.axis_index("req") % NX
    z_groups = [[z * NX + x for z in range(nz)] for x in range(NX)]
    keys = prefix_keys.reshape(span_count, span_len, width)
    values = prefix_values.reshape(span_count, span_len, width)
    per = steps // CHUNKS
    rows = per * heads

    named = block_table.reshape(-1)
    number = jnp.arange(named.shape[0], dtype=jnp.int32)
    goal = named // in_row
    before = (goal[:, None] == goal[None, :]) & (number[None, :] < number[:, None])
    rank = jnp.sum(before.astype(jnp.int32), axis=1)
    over = jnp.max((rank >= ROOM).astype(jnp.bfloat16))
    local_span = (named - column * span_count) % in_row

    def seats(low, room):
        inside = (rank >= low) & (rank < low + room)
        seat = jnp.where(inside, goal * room + rank - low, -1)
        taken = seat[None, :] == jnp.arange(nz * room, dtype=jnp.int32)[:, None]
        sender = jnp.sum(jnp.where(taken, number // depth, 0), axis=1)
        span_at = jnp.sum(jnp.where(taken, local_span + 1, 0), axis=1) - 1
        span_at = span_at.reshape(nz, room).astype(jnp.bfloat16)
        return sender, span_at, jnp.maximum(seat, 0).reshape(requests, depth)

    def along_z(array):
        return lax.all_to_all(
            array, "req", split_axis=0, concat_axis=0, tiled=True, axis_index_groups=z_groups
        )

    def send(part, sender, span_at):
        room = span_at.shape[1]
        lines = room * part.shape[1]
        outgoing = part[sender].reshape(nz, lines, width)
        extra = ((0, 0), (0, PAD - 1), (0, width - room))
        outgoing = jnp.concatenate([outgoing, jnp.pad(span_at[:, None, :], extra)], axis=1)
        incoming = along_z(outgoing)
        return incoming, incoming[:, lines, :room].astype(jnp.int32).reshape(-1)

    def packed(states, logs, note):
        lines = states.shape[1]
        logs = logs[:, :, : lines // logs.shape[1]].reshape(nz, lines)
        high = lax.reduce_precision(logs, 8, 7)
        middle = lax.reduce_precision(logs - high, 8, 7)
        logs = jnp.concatenate([high, middle, logs - high - middle], axis=1).astype(jnp.bfloat16)
        note = jnp.broadcast_to(note, (nz, PAD * width - 3 * lines))
        logs = jnp.concatenate([logs, note], axis=1).reshape(nz, PAD, width)
        return jnp.concatenate([states, logs], axis=1)

    def opened(states, slot_ids, rows):
        lines = states.shape[1] - PAD
        logs = states[:, lines:].reshape(nz, PAD * width).astype(jnp.float32)
        note = jnp.max(logs[:, -1])
        logs = logs[:, :lines] + logs[:, lines : 2 * lines] + logs[:, 2 * lines : 3 * lines]
        logs = logs.reshape(-1, rows)[slot_ids]
        parts = states[:, :lines].reshape(-1, rows, width)[slot_ids]
        return parts, logs, note

    sender, span_at, slot_ids = seats(0, ROOM)
    all_rows = steps * heads
    everything = queries.reshape(requests, all_rows, width)
    arrived, ids = send(everything, sender, span_at)

    def along_x(array, by):
        pairs = [(z * NX + x, z * NX + (x + by) % NX) for z in range(nz) for x in range(NX)]
        return lax.ppermute(array, "req", pairs)

    note = jnp.broadcast_to(over, (span_count, 2 * PAD, width))
    mine = jnp.concatenate([keys, values, note], axis=1)
    left = along_x(mine, 1)
    right = along_x(mine, -1)
    far_keys = along_x(left[:, :span_len], 1)
    far_rest = along_x(right[:, span_len:], -1)
    lacking = jnp.maximum(over, jnp.maximum(left[0, -1, 0], right[0, -1, 0]))
    lacking = jnp.maximum(lacking, far_rest[0, -1, 0])
    spans = (mine, right, far_keys, far_rest, left)

    def private():
        kv_local = new_keys.shape[2]
        grouped = queries.reshape(requests, steps, kv_local, heads // kv_local, width)
        own_part, own_log = own_states(
            grouped, suffix_keys, suffix_values, new_keys, new_values, suffix_len
        )
        own_part = own_part.reshape(requests, steps, heads, width)
        return own_part, own_log.reshape(requests, steps, heads)

    own_part, own_log = private()
    results = []
    held = []
    for c in range(CHUNKS):
        states, logs = row_states(ids, arrived, spans, ROOM, c * rows, rows, all_rows)
        states = packed(states, logs, lacking)
        states = along_z(states)
        held.append(states)
        if c > 0:
            states, results[-1] = lax.optimization_barrier((states, results[-1]))
        parts, logs, note = opened(states, slot_ids, rows)
        results.append(merge_own(parts, logs, own_part, own_log, c, per))

    def along_kv(merged):
        kv_count = lax.axis_size("kv")
        merged = merged.reshape(requests // kv_count, kv_count, steps, heads * width)
        return lax.all_to_all(merged, "kv", split_axis=1, concat_axis=3, tiled=True)

    def one_more_round(attended):
        room = in_row * CAP - ROOM
        sender, span_at, more_ids = seats(ROOM, room)
        incoming, ids = send(everything, sender, span_at)
        states, logs = row_states(ids, incoming, spans, room, 0, all_rows, all_rows)
        states = along_z(packed(states, logs, lacking))
        more, more_logs, _ = opened(states, more_ids, all_rows)
        late = (rank >= ROOM).reshape(requests, depth, 1)
        results = []
        own_part, own_log = private()
        for c, states in enumerate(held):
            parts, logs, _ = opened(states, slot_ids, rows)
            cut = slice(c * rows, (c + 1) * rows)
            parts = jnp.where(late[..., None], more[:, :, cut], parts)
            logs = jnp.where(late, more_logs[:, :, cut], logs)
            results.append(merge_own(parts, logs, own_part, own_log, c, per))
        return along_kv(jnp.concatenate(results, axis=1))

    attended = along_kv(jnp.concatenate(results, axis=1))
    return lax.cond(note > 0.0, one_more_round, lambda a: a, attended)


def solution(mesh):
    placed = (
        P("req", None, "kv", None),
        P("req", None, "kv", None),
        P("req", None, "kv", None),
        P("req", None, "kv", None),
        P("req", None, "kv", None),
        P("req"),
        P("req", None),
        P("req", None, "kv", None),
        P("req", None, "kv", None),
    )
    return jax.shard_map(
        local, mesh=mesh, in_specs=placed, out_specs=P("req", "kv", None, None), check_vma=False
    )
```
